256 devices in a mesh: seq: 64 (over z, x, y_lo), head: 4 (over y_hi, core).
Axes of the slice: x: 4, y: 4 (y_hi: 2, y_lo: 2; y = y_hi * 2 + y_lo), z: 8, core: 2. Of those that a mesh axis runs over, the one named last changes fastest.
Arguments:
- queries: bfloat16 [512, 64, 128], P('seq', 'head'), may hold values from -6 to 6
- shared_key_rows: bfloat16 [32768, 8, 128], P('seq', 'head'), may hold values from -10 to 10
- shared_value_rows: bfloat16 [32768, 8, 128], P('seq', 'head'), may hold values from -6 to 6
- tenant_key_rows: bfloat16 [262144, 8, 128], P('seq', 'head'), may hold values from -10 to 10
- tenant_value_rows: bfloat16 [262144, 8, 128], P('seq', 'head'), may hold values from -6 to 6
- tenant_ids: int32 [512], replicated, may hold values from 0 to 15, as said below
- tenant_len: int32 [16], replicated, may hold values from 4096 to 16384, as said below
- priv_len: int32 [512], P('seq'), may hold values from 0 to 1024, as said below
- page_table: int32 [512, 8], P('seq'), may hold values from 0 to 35, as said below
- private_key_pages: bfloat16 [2304, 128, 8, 128], P('seq', None, 'head'), may hold values from -12 to 12
- private_value_pages: bfloat16 [2304, 128, 8, 128], P('seq', None, 'head'), may hold values from -6 to 6
- out_weight: bfloat16 [8192, 8192], P('head', 'seq'), may hold values from -0.0625 to 0.0625
Outputs:
- attended_out: bfloat16 [512, 8192], P('head', 'seq')
The draws below stay inside these ranges and needn't reach their ends.
Inputs may be any that keep to these rules, and one draw needn't show every extreme that they name: `tenant_ids`: each tenant has at most 48 requests, and some tenant exactly 48. `tenant_len`: some tenant's prefix has exactly 16384 positions. `priv_len`: in each owner's block of 8 requests one has exactly 1024 private positions, and the block's requests together live on at most 36 pages. `page_table`: entries index the owner's own pool; the pages that hold live positions of an owner's requests are all different.
All inputs are finite; a program needn't handle non-finite values.
Results may differ from the reference program's by a relative error of at most 0.005.
Values may be sent and summed in bfloat16 or wider, within the bound.
A program may use at most 128 MiB of HBM per device.

```python
import math
import jax
import jax.numpy as jnp
from jax import lax

D = 8192
QUERY_HEADS = 64
KEY_VALUE_HEADS = 8
HEAD_SIZE = 128
OWNED_REQUESTS = 8
SHARED_SLICE = 512
PREFIX_LIMIT = 16384
PRIVATE_LIMIT = 1024
PAGE_POSITIONS = 128
MAXP = 8
OWNER_POOL_PAGES = 36
PREFIX_SLICE = 4096
REQUEST_COUNT = 512
TENANT_COUNT = 16
TCAP = 48
SHARED_LENGTH = 32768
N_SEQ = 64


def draw_queries(key, part):
    key = jax.random.fold_in(key, 11)
    value_rows = jnp.clip(jax.random.normal(key, (REQUEST_COUNT, QUERY_HEADS, HEAD_SIZE), jnp.float32), -6.0, 6.0)
    return value_rows.astype(jnp.bfloat16)


def draw_shared_key_rows(key, part):
    key = jax.random.fold_in(key, 12)
    value_rows = jnp.clip(2.5 * jax.random.normal(key, (SHARED_LENGTH, KEY_VALUE_HEADS, HEAD_SIZE), jnp.float32), -10.0, 10.0)
    return value_rows.astype(jnp.bfloat16)


def page_counts(key):
    owners = REQUEST_COUNT // OWNED_REQUESTS
    full_key, other_key = jax.random.split(key)
    favoured = jax.random.randint(full_key, (owners,), 0, OWNED_REQUESTS)
    others = jax.random.randint(other_key, (owners, OWNED_REQUESTS), 0, MAXP // 2 + 1)
    local = jnp.arange(OWNED_REQUESTS)
    return jnp.where(local[None, :] == favoured[:, None], MAXP, others)


def draw_priv_len(key, part):
    counts = page_counts(key)
    key = jax.random.fold_in(key, 21)
    tails = jax.random.randint(key, counts.shape, 1, PAGE_POSITIONS + 1)
    lengths = jnp.where(counts > 0, (counts - 1) * PAGE_POSITIONS + tails, 0)
    lengths = jnp.where(counts == MAXP, PRIVATE_LIMIT, lengths)
    return lengths.reshape(REQUEST_COUNT).astype(jnp.int32)


def draw_page_table(key, part):
    counts = page_counts(key)
    key = jax.random.fold_in(key, 22)
    owners = REQUEST_COUNT // OWNED_REQUESTS
    orders = jax.vmap(lambda single: jax.random.permutation(single, OWNER_POOL_PAGES))(jax.random.split(key, owners))
    offsets = jnp.cumsum(counts, axis=1) - counts
    places = (offsets[:, :, None] + jnp.arange(MAXP)[None, None, :]) % OWNER_POOL_PAGES
    page_lookup = jax.vmap(lambda order, place: order[place])(orders, places)
    return page_lookup.reshape(REQUEST_COUNT, MAXP).astype(jnp.int32)


def draw_tenant_len(key, part):
    key = jax.random.fold_in(key, 31)
    first_key, second_key = jax.random.split(key)
    lengths = jax.random.randint(first_key, (TENANT_COUNT,), PREFIX_LIMIT // 4, PREFIX_LIMIT + 1)
    favoured = jax.random.randint(second_key, (), 0, TENANT_COUNT)
    lengths = jnp.where(jnp.arange(TENANT_COUNT) == favoured, PREFIX_LIMIT, lengths)
    return lengths.astype(jnp.int32)


def draw_tenant_ids(key, part):
    key = jax.random.fold_in(key, 41)
    first_key, second_key, third_key = jax.random.split(key, 3)
    favoured = jax.random.randint(first_key, (), 0, TENANT_COUNT)
    slot_count = TENANT_COUNT * TCAP
    ranks = jax.random.permutation(second_key, slot_count)
    holders = jnp.arange(slot_count) // TCAP
    priority = jnp.where(holders == favoured, ranks - slot_count, ranks)
    chosen = jnp.argsort(priority, stable=True)[:REQUEST_COUNT]
    tenants = (chosen // TCAP)[jax.random.permutation(third_key, REQUEST_COUNT)]
    return tenants.astype(jnp.int32)


def shard_levels(own_key, extent, cuts, low, largest):
    level, own = 1.0, jax.random.fold_in(own_key, 6)
    for axis_at, parts in cuts:
        draws = jnp.exp(jax.random.uniform(jax.random.fold_in(own, axis_at), (parts,), jnp.float32, low / len(cuts), largest / len(cuts)))
        level = level * jnp.repeat(draws, extent[axis_at] // parts).reshape([-1 if axis == axis_at else 1 for axis in range(len(extent))])
    return level


def bell_draw(own_key, dims, width, bound, shards=(), held_as=jnp.bfloat16):
    values = jax.random.normal(own_key, dims, jnp.float32) * width
    if len(shards) > 0:
        values = shard_levels(own_key, dims, shards, -0.22, 0.18) * values
    return jnp.clip(values, min=-bound, max=bound).astype(held_as)


def setup_inputs(seed: int = 0) -> dict:
    key_of = jax.random.split(jax.random.key(seed), 13)
    queries = draw_queries(jax.random.fold_in(key_of[12], 71), 0)
    shared_key_rows = draw_shared_key_rows(jax.random.fold_in(key_of[12], 71), 0)
    shared_value_rows = bell_draw(key_of[2], (SHARED_LENGTH, KEY_VALUE_HEADS, HEAD_SIZE), 1.0, 6.0, ((0, 64), (1, 4)))
    tenant_key_rows = bell_draw(key_of[3], (TENANT_COUNT * PREFIX_LIMIT, KEY_VALUE_HEADS, HEAD_SIZE), 2.5, 10.0, ((0, 64), (1, 4)))
    tenant_value_rows = bell_draw(key_of[4], (TENANT_COUNT * PREFIX_LIMIT, KEY_VALUE_HEADS, HEAD_SIZE), 1.0, 6.0, ((0, 64), (1, 4)))
    tenant_ids = draw_tenant_ids(jax.random.fold_in(key_of[12], 71), 0)
    tenant_len = draw_tenant_len(jax.random.fold_in(key_of[12], 71), 0)
    priv_len = draw_priv_len(jax.random.fold_in(key_of[12], 71), 0)
    page_table = draw_page_table(jax.random.fold_in(key_of[12], 71), 0)
    private_key_pages = bell_draw(key_of[9], (OWNER_POOL_PAGES * N_SEQ, PAGE_POSITIONS, KEY_VALUE_HEADS, HEAD_SIZE), 3.0, 12.0, ((0, 64), (2, 4)))
    private_value_pages = bell_draw(key_of[10], (OWNER_POOL_PAGES * N_SEQ, PAGE_POSITIONS, KEY_VALUE_HEADS, HEAD_SIZE), 1.0, 6.0, ((0, 64), (2, 4)))
    out_weight = bell_draw(key_of[11], (QUERY_HEADS * HEAD_SIZE, D), (QUERY_HEADS * HEAD_SIZE) ** -0.5, 0.0625, ((0, 4), (1, 64)))
    return {"queries": queries, "shared_key_rows": shared_key_rows, "shared_value_rows": shared_value_rows, "tenant_key_rows": tenant_key_rows, "tenant_value_rows": tenant_value_rows, "tenant_ids": tenant_ids, "tenant_len": tenant_len, "priv_len": priv_len, "page_table": page_table, "private_key_pages": private_key_pages, "private_value_pages": private_value_pages, "out_weight": out_weight}


score_masked = -1e+30

def finish(scores, value_rows, usable, form):
    if usable is not None:
        scores = jnp.where(usable, scores, score_masked)
    maxima = lax.optimization_barrier(jnp.max(scores, axis=-1))
    weights = jnp.exp(scores - maxima[..., None])
    if usable is not None:
        weights = jnp.where(usable, weights, 0.0)
    totals = lax.optimization_barrier(jnp.sum(weights, axis=-1))
    rounded = lax.optimization_barrier(weights.astype(jnp.bfloat16))
    outputs = jnp.einsum(form, rounded.astype(jnp.float32), value_rows.astype(jnp.float32))
    return (maxima, totals, outputs)

def combine(earlier, later):
    highest = jnp.maximum(earlier[0], later[0])
    early_weight = jnp.exp(earlier[0] - highest)
    late_weight = jnp.exp(later[0] - highest)
    return (highest, early_weight * earlier[1] + late_weight * later[1], early_weight[..., None] * earlier[2] + late_weight[..., None] * later[2])

def reference(queries, shared_key_rows, shared_value_rows, tenant_key_rows, tenant_value_rows, tenant_ids, tenant_len, priv_len, page_table, private_key_pages, private_value_pages, out_weight):
    group_query_count = QUERY_HEADS // KEY_VALUE_HEADS
    factor = 1.0 / math.sqrt(HEAD_SIZE)
    group_rows = queries.reshape(REQUEST_COUNT, KEY_VALUE_HEADS, group_query_count, HEAD_SIZE)
    query_wide = group_rows.astype(jnp.float32)
    running_state = (jnp.full((REQUEST_COUNT, KEY_VALUE_HEADS, group_query_count), score_masked, jnp.float32), jnp.zeros((REQUEST_COUNT, KEY_VALUE_HEADS, group_query_count), jnp.float32), jnp.zeros((REQUEST_COUNT, KEY_VALUE_HEADS, group_query_count, HEAD_SIZE), jnp.float32))
    shared_key_slice = shared_key_rows.reshape(N_SEQ, SHARED_SLICE, KEY_VALUE_HEADS, HEAD_SIZE)
    shared_value_slice = shared_value_rows.reshape(N_SEQ, SHARED_SLICE, KEY_VALUE_HEADS, HEAD_SIZE)

    def shared_step(state, key_block):
        key_tile, value_tile = key_block
        scores = jnp.einsum('rkgd,tkd->rkgt', query_wide, key_tile.astype(jnp.float32)) * factor
        partial_out = finish(scores, value_tile, None, 'rkgt,tkd->rkgd')
        return (combine(state, partial_out), None)
    running_state, _ = lax.scan(shared_step, running_state, (shared_key_slice, shared_value_slice))
    tenant_key_slice = tenant_key_rows.reshape(TENANT_COUNT, 4, PREFIX_SLICE, KEY_VALUE_HEADS, HEAD_SIZE)
    tenant_value_slice = tenant_value_rows.reshape(TENANT_COUNT, 4, PREFIX_SLICE, KEY_VALUE_HEADS, HEAD_SIZE)

    def tenant_step(state, tenant):
        chosen = jnp.nonzero(tenant_ids == tenant, size=TCAP, fill_value=REQUEST_COUNT)[0]
        picked = jnp.minimum(chosen, REQUEST_COUNT - 1)
        tenant_queries = query_wide[picked]
        current = (state[0][picked], state[1][picked], state[2][picked])
        keys_here = lax.dynamic_index_in_dim(tenant_key_slice, tenant, 0, keepdims=False)
        values_here = lax.dynamic_index_in_dim(tenant_value_slice, tenant, 0, keepdims=False)
        length = tenant_len[tenant]
        for quarter in range(4):
            scores = jnp.einsum('rkgd,tkd->rkgt', tenant_queries, keys_here[quarter].astype(jnp.float32)) * factor
            places = quarter * PREFIX_SLICE + jnp.arange(PREFIX_SLICE, dtype=jnp.int32)
            usable = (places < length)[None, None, None, :]
            current = combine(current, finish(scores, values_here[quarter], usable, 'rkgt,tkd->rkgd'))
        state = tuple((whole.at[chosen].set(update, mode='drop') for whole, update in zip(state, current)))
        return (state, None)
    running_state, _ = lax.scan(tenant_step, running_state, jnp.arange(TENANT_COUNT, dtype=jnp.int32))
    pooled_key_rows = private_key_pages.reshape(N_SEQ, OWNER_POOL_PAGES, PAGE_POSITIONS, KEY_VALUE_HEADS, HEAD_SIZE)
    pooled_value_rows = private_value_pages.reshape(N_SEQ, OWNER_POOL_PAGES, PAGE_POSITIONS, KEY_VALUE_HEADS, HEAD_SIZE)
    tables = page_table.reshape(N_SEQ, OWNED_REQUESTS, MAXP)
    lengths = priv_len.reshape(N_SEQ, OWNED_REQUESTS)
    query_owned = query_wide.reshape(N_SEQ, OWNED_REQUESTS, KEY_VALUE_HEADS, group_query_count, HEAD_SIZE)

    def private_block(inputs):
        key_tile, value_tile, page_lookup, block_lengths, block_queries = inputs
        paged_key_rows = key_tile[page_lookup].reshape(OWNED_REQUESTS, PRIVATE_LIMIT, KEY_VALUE_HEADS, HEAD_SIZE)
        paged_value_rows = value_tile[page_lookup].reshape(OWNED_REQUESTS, PRIVATE_LIMIT, KEY_VALUE_HEADS, HEAD_SIZE)
        scores = jnp.einsum('rkgd,rtkd->rkgt', block_queries, paged_key_rows.astype(jnp.float32)) * factor
        usable = (jnp.arange(PRIVATE_LIMIT, dtype=jnp.int32)[None, :] < block_lengths[:, None])[:, None, None, :]
        return finish(scores, paged_value_rows, usable, 'rkgt,rtkd->rkgd')
    private_pieces = lax.map(private_block, (pooled_key_rows, pooled_value_rows, tables, lengths, query_owned))
    private_pieces = (private_pieces[0].reshape(REQUEST_COUNT, KEY_VALUE_HEADS, group_query_count), private_pieces[1].reshape(REQUEST_COUNT, KEY_VALUE_HEADS, group_query_count), private_pieces[2].reshape(REQUEST_COUNT, KEY_VALUE_HEADS, group_query_count, HEAD_SIZE))
    highest, totals, outputs = combine(running_state, private_pieces)
    attended = (outputs / totals[..., None]).astype(jnp.bfloat16).reshape(REQUEST_COUNT, QUERY_HEADS * HEAD_SIZE)
    return jnp.dot(attended, out_weight, preferred_element_type=jnp.float32).astype(jnp.bfloat16)
```

```python
import functools
import math

import jax
import jax.numpy as jnp
from jax import lax
from jax.experimental import pallas as pl
from jax.experimental.pallas import tpu as pltpu
from jax.sharding import PartitionSpec as P

MESH = pl.DeviceIdType.MESH
F32 = jnp.float32
BF16 = jnp.bfloat16
DEAD = -1e30
KV = 2
G = 8
D = 128
R = 8
HEADS = KV * G
CAP = 48
SLOTS = CAP * G
COLUMNS = R * G
LOG2E = math.log2(math.e)
SCALE = LOG2E / math.sqrt(D)


def dot(a, b):
    return jnp.dot(a, b, preferred_element_type=F32)


def dot_t(a, b):
    return lax.dot_general(a, b, (((1,), (1,)), ((), ())), preferred_element_type=F32)


def iota(shape, axis):
    return lax.broadcasted_iota(jnp.int32, shape, axis)


def kernel(
    NZ, NX, NH,
    q_hbm, sk_hbm, sv_hbm, tk_hbm, tv_hbm, ids_ref, tlen_ref, plen_ref, ptab_ref,
    pk_hbm, pv_hbm, w_hbm, out_ref,
    q_raw, q_wide, sk_raw, sv_raw, tk_raw, tv_raw, pk, pv, w,
    k_sh, v_sh, k_te, v_te,
    q_all, onehot, keys, qt_send, qt_recv,
    te_m, te_l, te_acc, to_send, to_recv, tl_send, tl_recv,
    te_hi, te_lo, te_stat, sh_o, sh_l,
    xo_send, xo_recv, xl_send, xl_recv,
    zo_send, zo_recv, zl_send, zl_recv,
    pr_o, pr_l, at, part, rs_recv,
    in_sem,
    qz_s, qz_r, qx_s, qx_r, pair_s, pair_r, xo_s, xo_r, xl_s, xl_r,
    zo_s, zo_r, zl_s, zl_r, az_s, az_r, ax_s, ax_r, rs_s, rs_r,
):
    seq = lax.axis_index("seq")
    h = lax.axis_index("head")
    b = lax.rem(seq, 2)
    x = lax.rem(seq // 2, NX)
    z = seq // (2 * NX)
    pages = pk.shape[0]
    zcols = NZ * COLUMNS
    zper = NZ // NH

    def seq_of(zz, xx, bb):
        return (zz * NX + xx) * 2 + bb

    def device(zz, xx, bb, hh):
        return {"seq": seq_of(zz, xx, bb), "head": hh}

    def z_of(dz):
        return lax.rem(z + dz + NZ, NZ)

    def x_of(dx):
        return lax.rem(x + dx + NX, NX)

    def h_of(dh):
        return lax.rem(h + dh + NH, NH)

    def b_of(db):
        return lax.rem(b + db, 2)

    def send(src, dst, s, r, dev):
        return pltpu.make_async_remote_copy(
            src_ref=src, dst_ref=dst, send_sem=s, recv_sem=r, device_id=dev, device_id_type=MESH
        )

    me = device(z, x, b, h)
    pair = device(z, x, b_of(1), h)
    started = []

    def go(*args):
        copy = send(*args)
        copy.start()
        started.append(copy)

    def arrived(ref, s, r):
        send(ref, ref, s, r, pair).wait_recv()

    loads = {}
    for at_sem, (name, src, dst) in enumerate((
        ("q", q_hbm, q_raw),
        ("tk", tk_hbm, tk_raw),
        ("sk", sk_hbm, sk_raw.at[0]),
        ("sv", sv_hbm, sv_raw.at[0]),
        ("tv", tv_hbm, tv_raw),
        ("pk", pk_hbm, pk),
        ("pv", pv_hbm, pv),
        ("w", w_hbm, w.at[0]),
    )):
        loads[name] = pltpu.make_async_copy(src, dst, in_sem.at[at_sem])
        loads[name].start()

    barrier = pltpu.get_barrier_semaphore()
    peers = [device(z_of(dz), x, b, h) for dz in range(1, NZ)]
    peers += [device(z, x_of(dx), b, h) for dx in range(1, NX)]
    peers += [
        device(z, x, b_of(db), h_of(dh)) for dh in range(NH) for db in range(2) if dh + db > 0
    ]
    for peer in peers:
        pl.semaphore_signal(barrier, inc=1, device_id=peer, device_id_type=MESH)

    loads["q"].wait()
    q_wide[...] = q_raw[...].astype(F32).reshape(R * HEADS, D)
    q_all[x, z] = jnp.concatenate(
        [q_wide[pl.ds(i, R, stride=HEADS), :] for i in range(HEADS)], axis=0
    ).astype(BF16)

    pl.semaphore_wait(barrier, len(peers))

    for dz in range(1, NZ):
        go(q_all.at[x, z], q_all.at[x, z], qz_s.at[dz - 1], qz_r.at[dz - 1], device(z_of(dz), x, b, h))
    go(sk_hbm, sk_raw.at[1], pair_s.at[0], pair_r.at[0], pair)
    go(sv_hbm, sv_raw.at[1], pair_s.at[1], pair_r.at[1], pair)

    row, col = iota((2 * D, 2 * D), 0), iota((2 * D, 2 * D), 1)
    sort = (col == jnp.where(row < D, 2 * row, 2 * (row - D) + 1)).astype(F32).astype(BF16)

    def sort_keys(raw, into, count, base):
        def step(i, carry):
            at_row = pl.multiple_of(i * 2 * D, 2 * D)
            to_row = pl.multiple_of(base + i * D, D)
            rows = dot(sort, raw[pl.ds(at_row, 2 * D), :]).astype(BF16)
            into[0, pl.ds(to_row, D), :] = rows[:D]
            into[1, pl.ds(to_row, D), :] = rows[D:]
            return carry

        lax.fori_loop(0, count // D, step, 0, unroll=4)

    def sort_values(raw, into, count, base):
        def step(i, carry):
            at_row = pl.multiple_of(i * 2 * D, 2 * D)
            to_row = pl.multiple_of(base + i * D, D)
            rows = dot(sort, raw[pl.ds(at_row, 2 * D), :])
            into[0, :, pl.ds(to_row, D)] = rows[:D].T.astype(BF16)
            into[1, :, pl.ds(to_row, D)] = rows[D:].T.astype(BF16)
            return carry

        lax.fori_loop(0, count // D, step, 0, unroll=4)

    positions = k_te.shape[1]
    half = sk_raw.shape[1] // 2

    tenant = seq // 4
    requests = ids_ref.shape[1]
    match = (ids_ref[...] == tenant).astype(F32)
    match = jnp.broadcast_to(match, (16, requests))
    upto = (iota((requests, requests), 0) <= iota((requests, requests), 1)).astype(F32).astype(BF16)
    slot = (match * dot(match.astype(BF16), upto)).astype(BF16)
    for xx in range(NX):
        j = iota((1, zcols), 1)
        request = ((j // COLUMNS * NX + xx) * 2 + b) * R + lax.rem(j, R)
        pick = (iota((requests, zcols), 0) == request).astype(F32).astype(BF16)
        found = dot(slot, pick)[:1]
        group = (lax.rem(j, COLUMNS) // R).astype(F32)
        key = jnp.where(found > 0.5, group * CAP + found - 1.0, -1.0)
        keys[xx] = jnp.broadcast_to(key, (8, zcols))
        onehot[xx] = (iota((SLOTS, zcols), 0).astype(F32) == key).astype(F32).astype(BF16)

    for dz in range(1, NZ):
        arrived(q_all.at[x, z_of(-dz)], qz_s.at[dz - 1], qz_r.at[dz - 1])
    for dx in range(1, NX):
        go(q_all.at[x], q_all.at[x], qx_s.at[dx - 1], qx_r.at[dx - 1], device(z, x_of(dx), b, h))

    loads["tk"].wait()
    sort_keys(tk_raw, k_te, positions, 0)
    loads["sk"].wait()
    sort_keys(sk_raw.at[0], k_sh, half, 0)
    loads["sv"].wait()
    sort_values(sv_raw.at[0], v_sh, half, 0)
    loads["tv"].wait()
    sort_values(tv_raw, v_te, positions, 0)

    for dx in range(1, NX):
        arrived(q_all.at[x_of(-dx)], qx_s.at[dx - 1], qx_r.at[dx - 1])

    def chunk_queries(xx, kv):
        return q_all[xx, :, kv * COLUMNS:(kv + 1) * COLUMNS, :].reshape(zcols, D)

    for kv in range(KV):
        total = dot(onehot[0], chunk_queries(0, kv))
        for xx in range(1, NX):
            total += dot(onehot[xx], chunk_queries(xx, kv))
        qt_send[kv] = total.astype(BF16)
    go(qt_send, qt_recv, pair_s.at[2], pair_r.at[2], pair)

    loads["pk"].wait()
    loads["pv"].wait()
    span = ptab_ref.shape[1] * pk.shape[1]
    lane = iota((HEADS, span), 1)
    own = lax.rem(lane, 2) == iota((HEADS, span), 0) // G
    for r in range(R):
        keys_here = jnp.concatenate([pk[ptab_ref[r, p]] for p in range(ptab_ref.shape[1])], axis=0)
        values_here = jnp.concatenate([pv[ptab_ref[r, p]] for p in range(ptab_ref.shape[1])], axis=0)
        s = dot_t(q_raw[r], keys_here)
        s = jnp.where(own & (lane // 2 < plen_ref[r]), s, DEAD)
        m = jnp.max(s, axis=1, keepdims=True)
        p = jnp.exp2((s - m) * SCALE)
        l = jnp.sum(p, axis=1, keepdims=True)
        o = dot(p.astype(BF16), values_here) / l
        lse = jnp.where(plen_ref[r] > 0, m * SCALE + jnp.log2(l), DEAD)
        pr_o[pl.ds(r, HEADS, stride=R), :] = o
        pr_l[pl.ds(r, HEADS, stride=R), :] = jnp.broadcast_to(lse, (HEADS, D))

    arrived(sk_raw.at[1], pair_s.at[0], pair_r.at[0])
    sort_keys(sk_raw.at[1], k_sh, half, half)
    arrived(sv_raw.at[1], pair_s.at[1], pair_r.at[1])
    sort_values(sv_raw.at[1], v_sh, half, half)

    arrived(qt_recv, pair_s.at[2], pair_r.at[2])
    extent = tlen_ref[tenant] - lax.rem(seq, 4) * positions
    block = min(1024, positions)
    for kv in range(KV):
        queries = (qt_send[kv].astype(F32) + qt_recv[kv].astype(F32)).astype(BF16)
        te_m[...] = jnp.full(te_m.shape, DEAD, F32)
        te_l[...] = jnp.zeros(te_l.shape, F32)
        te_acc[...] = jnp.zeros(te_acc.shape, F32)

        def step(i, carry):
            base = pl.multiple_of(i * block, block)
            s = dot_t(k_te[kv, pl.ds(base, block), :], queries)
            s = jnp.where(iota((block, SLOTS), 0) < extent - base, s, DEAD)
            m_old = te_m[:1]
            m = jnp.maximum(m_old, jnp.max(s, axis=0, keepdims=True))
            p = jnp.exp2((s - m) * SCALE)
            keep = jnp.exp2((m_old - m) * SCALE)
            te_m[:1] = m
            te_l[:1] = te_l[:1] * keep + jnp.sum(p, axis=0, keepdims=True)
            te_acc[...] = te_acc[...] * keep + dot(v_te[kv, :, pl.ds(base, block)], p.astype(BF16))
            return carry

        lax.fori_loop(0, positions // block, step, 0)
        l = te_l[:1]
        to_send[kv] = (te_acc[...] / l).astype(BF16)
        lse = jnp.where(extent > 0, te_m[:1] * SCALE + jnp.log2(l), DEAD)
        tl_send[kv] = jnp.broadcast_to(lse, (8, SLOTS))
    go(to_send, to_recv, pair_s.at[3], pair_r.at[3], pair)
    go(tl_send, tl_recv, pair_s.at[4], pair_r.at[4], pair)
    go(w_hbm, w.at[1], pair_s.at[5], pair_r.at[5], pair)

    width = min(256, zcols)

    def shared(xx):
        for kv in range(KV):
            for c in range(0, zcols, width):
                zs = slice(c // COLUMNS, (c + width) // COLUMNS)
                queries = q_all[xx, zs, kv * COLUMNS:(kv + 1) * COLUMNS, :].reshape(width, D)
                s = dot_t(k_sh[kv], queries)
                m = jnp.max(s, axis=0, keepdims=True)
                p = jnp.exp2((s - m) * SCALE)
                l = jnp.sum(p, axis=0, keepdims=True)
                sh_o[xx, kv, :, c:c + width] = dot(v_sh[kv], p.astype(BF16)) / l
                lse = m * SCALE + jnp.log2(l)
                sh_l[xx, kv, :, c:c + width] = jnp.broadcast_to(lse, (8, width))

    def tenants():
        arrived(to_recv, pair_s.at[3], pair_r.at[3])
        arrived(tl_recv, pair_s.at[4], pair_r.at[4])
        for kv in range(KV):
            l1, l2 = tl_send[kv][:1], tl_recv[kv][:1]
            top = jnp.maximum(l1, l2)
            w1, w2 = jnp.exp2(l1 - top), jnp.exp2(l2 - top)
            whole = w1 + w2
            o = to_send[kv].astype(F32) * (w1 / whole) + to_recv[kv].astype(F32) * (w2 / whole)
            hi = o.astype(BF16)
            te_hi[kv] = hi
            te_lo[kv] = (o - hi.astype(F32)).astype(BF16)
            rest = top + jnp.log2(whole)
            terms = []
            for _ in range(3):
                term = rest.astype(BF16).astype(F32)
                terms.append(term)
                rest = rest - term
            terms.append(jnp.zeros((13, SLOTS), F32))
            te_stat[kv] = jnp.concatenate(terms, axis=0).astype(BF16)

    def merge(xx):
        for kv in range(KV):
            spread = onehot[xx]
            stat = dot(te_stat[kv], spread)
            l2 = stat[0:1] + stat[1:2] + stat[2:3]
            l2 = jnp.where(keys[xx][:1] >= 0.0, l2, DEAD)
            l1 = sh_l[xx, kv][:1]
            top = jnp.maximum(l1, l2)
            w1, w2 = jnp.exp2(l1 - top), jnp.exp2(l2 - top)
            whole = w1 + w2
            o2 = dot(te_hi[kv], spread) + dot(te_lo[kv], spread)
            o = sh_o[xx, kv] * (w1 / whole) + o2 * (w2 / whole)
            xo_send[xx, kv] = o.astype(BF16)
            xl_send[xx, kv] = jnp.broadcast_to(top + jnp.log2(whole), (8, zcols))

    def dispatch(dx):
        to = device(z, x_of(dx), b, h)
        go(xo_send.at[x_of(dx)], xo_recv.at[dx - 1], xo_s.at[dx - 1], xo_r.at[dx - 1], to)
        go(xl_send.at[x_of(dx)], xl_recv.at[dx - 1], xl_s.at[dx - 1], xl_r.at[dx - 1], to)

    ahead = min(2, NX - 1)
    for dx in range(1, ahead + 1):
        shared(x_of(dx))
    tenants()
    for dx in range(1, ahead + 1):
        merge(x_of(dx))
        dispatch(dx)
    for dx in range(ahead + 1, NX):
        shared(x_of(dx))
        merge(x_of(dx))
        dispatch(dx)
    shared(x)
    merge(x)

    for dx in range(1, NX):
        arrived(xo_recv.at[dx - 1], xo_s.at[dx - 1], xo_r.at[dx - 1])
        arrived(xl_recv.at[dx - 1], xl_s.at[dx - 1], xl_r.at[dx - 1])

    def combine(pieces):
        top = pieces[0][0]
        for lse, _ in pieces[1:]:
            top = jnp.maximum(top, lse)
        weights = [jnp.exp2(lse - top) for lse, _ in pieces]
        whole = functools.reduce(lambda one, two: one + two, weights)
        total = None
        for weight, (_, o) in zip(weights, pieces):
            term = o().astype(F32) * (weight / whole)
            total = term if total is None else total + term
        return total, top + jnp.log2(whole)

    both = 2 * COLUMNS
    low = iota((D, both), 1) < COLUMNS
    for c in range(0, zcols, both):
        cut = slice(c, c + both)
        halves, marks = [], []
        for kv in range(KV):
            pieces = [(xl_send[x, kv, :1, cut], lambda: xo_send[x, kv, :, cut])]
            for dx in range(1, NX):
                pieces.append((
                    xl_recv[dx - 1, kv, :1, cut],
                    lambda dx=dx: xo_recv[dx - 1, kv, :, cut],
                ))
            o, lse = combine(pieces)
            halves.append(o)
            marks.append(jnp.broadcast_to(lse, (8, both)))
        zz = c // COLUMNS
        zo_send[zz] = jnp.where(low, halves[0], pltpu.roll(halves[1], COLUMNS, 1)).astype(BF16)
        zo_send[zz + 1] = jnp.where(low, pltpu.roll(halves[0], COLUMNS, 1), halves[1]).astype(BF16)
        zl_send[zz] = jnp.where(low[:8], marks[0], pltpu.roll(marks[1], COLUMNS, 1))
        zl_send[zz + 1] = jnp.where(low[:8], pltpu.roll(marks[0], COLUMNS, 1), marks[1])
    for dz in range(1, NZ):
        to = device(z_of(dz), x, b, h)
        go(zo_send.at[z_of(dz)], zo_recv.at[dz - 1], zo_s.at[dz - 1], zo_r.at[dz - 1], to)
        go(zl_send.at[z_of(dz)], zl_recv.at[dz - 1], zl_s.at[dz - 1], zl_r.at[dz - 1], to)

    private_o = pr_o[...].T
    private_l = pr_l[...].T[:1]
    for dz in range(1, NZ):
        arrived(zo_recv.at[dz - 1], zo_s.at[dz - 1], zo_r.at[dz - 1])
        arrived(zl_recv.at[dz - 1], zl_s.at[dz - 1], zl_r.at[dz - 1])
    pieces = [(private_l, lambda: private_o), (zl_send[z][:1], lambda: zo_send[z])]
    for dz in range(1, NZ):
        pieces.append((zl_recv[dz - 1][:1], lambda dz=dz: zo_recv[dz - 1]))
    attended, _ = combine(pieces)
    at[x, z] = attended.T.astype(BF16)

    for dz in range(1, NZ):
        go(at.at[x, z], at.at[x, z], az_s.at[dz - 1], az_r.at[dz - 1], device(z_of(dz), x, b, h))
    for dz in range(1, NZ):
        arrived(at.at[x, z_of(-dz)], az_s.at[dz - 1], az_r.at[dz - 1])
    for dx in range(1, NX):
        go(at.at[x], at.at[x], ax_s.at[dx - 1], ax_r.at[dx - 1], device(z, x_of(dx), b, h))

    def project(xx):
        wide = at[xx].astype(F32)
        rows = [
            wide[:, i * R:(i + 1) * R, :].reshape(NZ * R, D).astype(BF16) for i in range(HEADS)
        ]
        rows = jnp.concatenate(rows, axis=1)
        for db in range(2):
            part[db, :, xx] = dot(rows, w[db]).reshape(NZ, R, D)

    loads["w"].wait()
    arrived(w.at[1], pair_s.at[5], pair_r.at[5])
    project(x)
    for dx in range(1, NX):
        arrived(at.at[x_of(-dx)], ax_s.at[dx - 1], ax_r.at[dx - 1])
        project(x_of(-dx))

    for k in range(1, 2 * NH):
        dh, db = k // 2, k % 2
        src = part.at[db, pl.ds(h_of(dh) * zper, zper)]
        go(src, rs_recv.at[k - 1], rs_s.at[k - 1], rs_r.at[k - 1], device(z, x, b_of(db), h_of(dh)))
    totals = [part[0, pl.ds(h * zper, zper)], None]
    for k in range(1, 2 * NH):
        arrived(rs_recv.at[k - 1], rs_s.at[k - 1], rs_r.at[k - 1])
        got = rs_recv[k - 1]
        totals[k % 2] = got if totals[k % 2] is None else totals[k % 2] + got
    first = jnp.where(b == 0, totals[0], totals[1])
    second = jnp.where(b == 0, totals[1], totals[0])
    rows = jnp.concatenate([first[:, :, None], second[:, :, None]], axis=2)
    out_ref[...] = rows.reshape(zper * NX * 2 * R, D).astype(BF16)

    for copy in started:
        copy.wait_send()


def local(NZ, NX, NH, queries, sk, sv, tk, tv, ids, tlen, plen, ptab, pk, pv, w):
    flat = lambda rows: rows.reshape(rows.shape[0] * KV, D)
    paged = lambda rows: rows.reshape(rows.shape[0], rows.shape[1] * KV, D)
    sk, sv, tk, tv = flat(sk), flat(sv), flat(tk), flat(tv)
    pk, pv = paged(pk), paged(pv)
    shared2, positions = sk.shape[0], tk.shape[0] // KV
    zcols = NZ * COLUMNS
    zper = NZ // NH
    dma = pltpu.SemaphoreType.DMA
    v = pltpu.VMEM
    scratch = [
        v(queries.shape, BF16), v((R * HEADS, D), F32),
        v((2, shared2, D), BF16), v((2, shared2, D), BF16), v(tk.shape, BF16), v(tv.shape, BF16),
        v(pk.shape, BF16), v(pv.shape, BF16), v((2,) + w.shape, BF16),
        v((KV, shared2, D), BF16), v((KV, D, shared2), BF16),
        v((KV, positions, D), BF16), v((KV, D, positions), BF16),
        v((NX, NZ, R * HEADS, D), BF16), v((NX, SLOTS, zcols), BF16), v((NX, 8, zcols), F32),
        v((KV, SLOTS, D), BF16), v((KV, SLOTS, D), BF16),
        v((8, SLOTS), F32), v((8, SLOTS), F32), v((D, SLOTS), F32),
        v((KV, D, SLOTS), BF16), v((KV, D, SLOTS), BF16),
        v((KV, 8, SLOTS), F32), v((KV, 8, SLOTS), F32),
        v((KV, D, SLOTS), BF16), v((KV, D, SLOTS), BF16), v((KV, 16, SLOTS), BF16),
        v((NX, KV, D, zcols), F32), v((NX, KV, 8, zcols), F32),
        v((NX, KV, D, zcols), BF16), v((NX - 1, KV, D, zcols), BF16),
        v((NX, KV, 8, zcols), F32), v((NX - 1, KV, 8, zcols), F32),
        v((NZ, D, R * HEADS), BF16), v((NZ - 1, D, R * HEADS), BF16),
        v((NZ, 8, R * HEADS), F32), v((NZ - 1, 8, R * HEADS), F32),
        v((R * HEADS, D), F32), v((R * HEADS, D), F32),
        v((NX, NZ, R * HEADS, D), BF16), v((2, NZ, NX, R, D), F32),
        v((2 * NH - 1, zper, NX, R, D), F32),
        dma((8,)),
    ]
    for count in (NZ - 1, NX - 1, 6, NX - 1, NX - 1, NZ - 1, NZ - 1, NZ - 1, NX - 1, 2 * NH - 1):
        scratch += [dma((count,)), dma((count,))]
    hbm = pl.BlockSpec(memory_space=pl.ANY)
    smem = pl.BlockSpec(memory_space=pltpu.SMEM)
    vmem = pl.BlockSpec(memory_space=pltpu.VMEM)
    return pl.pallas_call(
        functools.partial(kernel, NZ, NX, NH),
        out_shape=jax.ShapeDtypeStruct((zper * NX * 2 * R, D), BF16),
        in_specs=[hbm] * 5 + [vmem, smem, smem, smem] + [hbm] * 3,
        out_specs=vmem,
        scratch_shapes=scratch,
        compiler_params=pltpu.CompilerParams(
            collective_id=0, has_side_effects=True, vmem_limit_bytes=56 * 1024 * 1024
        ),
    )(queries, sk, sv, tk, tv, ids.reshape(1, -1), tlen, plen, ptab, pk, pv, w)


def solution(mesh):
    sizes = dict(mesh.shape)
    NX = 4 if sizes["seq"] == 64 else 2
    NZ = sizes["seq"] // (2 * NX)
    placed = (
        P("seq", "head", None),
        P("seq", "head", None),
        P("seq", "head", None),
        P("seq", "head", None),
        P("seq", "head", None),
        P(),
        P(),
        P("seq"),
        P("seq", None),
        P("seq", None, "head", None),
        P("seq", None, "head", None),
        P("head", "seq"),
    )
    return jax.shard_map(
        functools.partial(local, NZ, NX, sizes["head"]),
        mesh=mesh, in_specs=placed, out_specs=P("head", "seq"), check_vma=False,
    )
```

```python
import functools
import math

import jax
import jax.numpy as jnp
from jax import lax
from jax.experimental import pallas as pl
from jax.experimental.pallas import tpu as pltpu
from jax.sharding import PartitionSpec as P

MESH = pl.DeviceIdType.MESH
F32 = jnp.float32
BF16 = jnp.bfloat16
DEAD = -1e30
KV = 2
G = 8
D = 128
R = 8
HEADS = KV * G
STAT = 16
CAP = 48
SLOTS = CAP * G
COLUMNS = R * G
LOG2E = math.log2(math.e)
SCALE = LOG2E / math.sqrt(D)


def dot(a, b):
    return jnp.dot(a, b, preferred_element_type=F32)


def dot_t(a, b):
    return lax.dot_general(a, b, (((1,), (1,)), ((), ())), preferred_element_type=F32)


def split3(v):
    terms = []
    for _ in range(3):
        term = v.astype(BF16).astype(F32)
        terms.append(term)
        v = v - term
    terms.append(jnp.zeros((STAT - 3, v.shape[1]), F32))
    return jnp.concatenate(terms, axis=0).astype(BF16)


def join3(rows):
    rows = rows.astype(F32)
    return rows[0:1] + rows[1:2] + rows[2:3]


def combine(pieces):
    top = pieces[0][0]
    for lse, _ in pieces[1:]:
        top = jnp.maximum(top, lse)
    weights = [jnp.exp2(lse - top) for lse, _ in pieces]
    whole = functools.reduce(lambda one, two: one + two, weights)
    inverse = 1.0 / whole
    total = None
    for weight, (_, o) in zip(weights, pieces):
        term = o().astype(F32) * (weight * inverse)
        total = term if total is None else total + term
    return total, top + jnp.log2(whole)


def iota(shape, axis):
    return lax.broadcasted_iota(jnp.int32, shape, axis)


def kernel(
    NZ, NX, NH,
    q_hbm, sk_hbm, sv_hbm, tk_hbm, tv_hbm, ids_ref, tlen_ref, plen_ref, ptab_ref,
    pk_hbm, pv_hbm, w_hbm, out_ref,
    q_raw, q_wide, sk_raw, sv_raw, tk_raw, tv_raw, pk, pv, w,
    k_sh, v_sh, k_te, v_te,
    q_all, onehot, keys, qt_send, qt_recv,
    te_m, te_l, te_acc, to_send, to_recv, tl_send, tl_recv,
    te_hi, te_lo, te_stat, sh_o, sh_l,
    xo_send, xo_half, xo_full, zo_own, zl_own, zo_send, zo_recv,
    pr_o, pr_l, at, part, rs_recv,
    in_sem,
    qz_s, qz_r, qx_s, qx_r, pair_s, pair_r, xo_s, xo_r,
    zo_s, zo_r, az_s, az_r, ax_s, ax_r, rs_s, rs_r,
):
    seq = lax.axis_index("seq")
    h = lax.axis_index("head")
    b = lax.rem(seq, 2)
    x = lax.rem(seq // 2, NX)
    z = seq // (2 * NX)
    pages = pk.shape[0]
    zcols = NZ * COLUMNS
    zper = NZ // NH

    def seq_of(zz, xx, bb):
        return (zz * NX + xx) * 2 + bb

    def device(zz, xx, bb, hh):
        return {"seq": seq_of(zz, xx, bb), "head": hh}

    zorder = [(p + 1) // 2 if p % 2 else -(p // 2) for p in range(NZ)]
    xorder = [0, 1, -1, 2]
    cuts = [0, 1, 3, 5, 8] if NZ == 8 else [0, 1, NZ]
    groups = list(zip(cuts[:-1], cuts[1:]))

    def back(p):
        return [(zorder[p] + other) % NZ for other in zorder].index(0)

    def z_of(dz):
        return lax.rem(z + dz + NZ, NZ)

    def x_of(dx):
        return lax.rem(x + dx + NX, NX)

    def h_of(dh):
        return lax.rem(h + dh + NH, NH)

    def b_of(db):
        return lax.rem(b + db, 2)

    def send(src, dst, s, r, dev):
        return pltpu.make_async_remote_copy(
            src_ref=src, dst_ref=dst, send_sem=s, recv_sem=r, device_id=dev, device_id_type=MESH
        )

    me = device(z, x, b, h)
    pair = device(z, x, b_of(1), h)
    started = []

    def go(*args):
        copy = send(*args)
        copy.start()
        started.append(copy)

    def arrived(ref, s, r):
        send(ref, ref, s, r, pair).wait_recv()

    loads = {}
    for at_sem, (name, src, dst) in enumerate((
        ("q", q_hbm, q_raw),
        ("tk", tk_hbm, tk_raw),
        ("sk", sk_hbm, sk_raw.at[0]),
        ("sv", sv_hbm, sv_raw.at[0]),
        ("tv", tv_hbm, tv_raw),
        ("pk", pk_hbm, pk),
        ("pv", pv_hbm, pv),
        ("w", w_hbm, w.at[0]),
    )):
        loads[name] = pltpu.make_async_copy(src, dst, in_sem.at[at_sem])
        loads[name].start()

    barrier = pltpu.get_barrier_semaphore()
    peers = [device(z_of(dz), x, b, h) for dz in range(1, NZ)]
    peers += [device(z, x_of(dx), b, h) for dx in range(1, NX)]
    peers += [
        device(z, x, b_of(db), h_of(dh)) for dh in range(NH) for db in range(2) if dh + db > 0
    ]
    for peer in peers:
        pl.semaphore_signal(barrier, inc=1, device_id=peer, device_id_type=MESH)

    loads["q"].wait()
    q_wide[...] = q_raw[...].astype(F32).reshape(R * HEADS, D)
    q_all[0, 0] = jnp.concatenate(
        [q_wide[pl.ds(i, R, stride=HEADS), :] for i in range(HEADS)], axis=0
    ).astype(BF16)

    pl.semaphore_wait(barrier, len(peers))

    left, right = device(z, x_of(-1), b, h), device(z, x_of(1), b, h)

    def z_start(buf, zs, zr):
        for p in range(1, NZ):
            q = back(p)
            go(buf.at[0, 0], buf.at[0, q], zs.at[p - 1], zr.at[q - 1], device(z_of(zorder[p]), x, b, h))

    def z_wait(buf, zs, zr, group):
        for p in range(*groups[group]):
            if p > 0:
                arrived(buf.at[0, p], zs.at[p - 1], zr.at[p - 1])

    def block(buf, slot, group, kind=None):
        first, last = groups[group]
        if kind is None:
            return buf.at[slot, pl.ds(first, last - first)]
        return buf.at[slot, pl.ds(first, last - first), pl.ds((kind - 2) * COLUMNS, COLUMNS)]

    def forward(buf, xs, xr, group):
        k = 4 * group
        go(block(buf, 0, group), block(buf, 2, group), xs.at[k], xr.at[k], right)
        go(block(buf, 0, group), block(buf, 1, group), xs.at[k + 1], xr.at[k + 1], left)

    def relay(buf, xs, xr, group):
        k = 4 * group
        arrived(block(buf, 2, group), xs.at[k], xr.at[k])
        go(block(buf, 2, group, 2), block(buf, 3, group, 2), xs.at[k + 2], xr.at[k + 2], right)
        arrived(block(buf, 1, group), xs.at[k + 1], xr.at[k + 1])
        go(block(buf, 1, group, 3), block(buf, 3, group, 3), xs.at[k + 3], xr.at[k + 3], left)

    def far_wait(buf, xs, xr, group):
        for kind in (2, 3):
            k = 4 * group + kind
            arrived(block(buf, 3, group, kind), xs.at[k], xr.at[k])

    q_line = (q_all, qx_s, qx_r)
    z_start(q_all, qz_s, qz_r)
    forward(*q_line, 0)
    go(sk_hbm, sk_raw.at[1], pair_s.at[0], pair_r.at[0], pair)
    go(sv_hbm, sv_raw.at[1], pair_s.at[1], pair_r.at[1], pair)

    row, col = iota((2 * D, 2 * D), 0), iota((2 * D, 2 * D), 1)
    sort = (col == jnp.where(row < D, 2 * row, 2 * (row - D) + 1)).astype(F32).astype(BF16)

    def sort_keys(raw, into, first, last, base):
        def step(i, carry):
            at_row = pl.multiple_of(i * 2 * D, 2 * D)
            to_row = pl.multiple_of(base + i * D, D)
            rows = dot(sort, raw[pl.ds(at_row, 2 * D), :]).astype(BF16)
            into[0, pl.ds(to_row, D), :] = rows[:D]
            into[1, pl.ds(to_row, D), :] = rows[D:]
            return carry

        lax.fori_loop(first // D, last // D, step, 0, unroll=4)

    def sort_values(raw, into, first, last, base):
        def step(i, carry):
            at_row = pl.multiple_of(i * 2 * D, 2 * D)
            to_row = pl.multiple_of(base + i * D, D)
            rows = dot(sort, raw[pl.ds(at_row, 2 * D), :])
            into[0, :, pl.ds(to_row, D)] = rows[:D].T.astype(BF16)
            into[1, :, pl.ds(to_row, D)] = rows[D:].T.astype(BF16)
            return carry

        lax.fori_loop(first // D, last // D, step, 0, unroll=4)

    positions = k_te.shape[1]
    half = sk_raw.shape[1] // 2

    tenant = seq // 4
    requests = ids_ref.shape[1]
    match = (ids_ref[...] == tenant).astype(F32)
    match = jnp.broadcast_to(match, (16, requests))
    upto = (iota((requests, requests), 0) <= iota((requests, requests), 1)).astype(F32).astype(BF16)
    slot = (match * dot(match.astype(BF16), upto)).astype(BF16)

    def mark(xx):
        j = iota((1, zcols), 1)
        place = j // COLUMNS
        away = jnp.where(place % 2 == 1, (place + 1) // 2, -(place // 2))
        owner = seq_of(lax.rem(z + away + NZ, NZ), x_of(xorder[xx]), b)
        request = owner * R + lax.rem(j, R)
        pick = (iota((requests, zcols), 0) == request).astype(F32).astype(BF16)
        found = dot(slot, pick)[:1]
        group = (lax.rem(j, COLUMNS) // R).astype(F32)
        key = jnp.where(found > 0.5, group * CAP + found - 1.0, -1.0)
        keys[xx] = jnp.broadcast_to(key, (8, zcols))
        onehot[xx] = (iota((SLOTS, zcols), 0).astype(F32) == key).astype(F32).astype(BF16)

    def private(r):
        keys_here = jnp.concatenate([pk[ptab_ref[r, p]] for p in range(ptab_ref.shape[1])], axis=0)
        values_here = jnp.concatenate([pv[ptab_ref[r, p]] for p in range(ptab_ref.shape[1])], axis=0)
        s = dot_t(q_raw[r], keys_here)
        s = jnp.where(own & (lane // 2 < plen_ref[r]), s, DEAD)
        m = jnp.max(s, axis=1, keepdims=True)
        p = jnp.exp2((s - m) * SCALE)
        l = jnp.sum(p, axis=1, keepdims=True)
        o = dot(p.astype(BF16), values_here) / l
        lse = jnp.where(plen_ref[r] > 0, m * SCALE + jnp.log2(l), DEAD)
        pr_o[pl.ds(r, HEADS, stride=R), :] = o
        pr_l[pl.ds(r, HEADS, stride=R), :] = jnp.broadcast_to(lse, (HEADS, D))

    span = ptab_ref.shape[1] * pk.shape[1]
    lane = iota((HEADS, span), 1)
    own = lax.rem(lane, 2) == iota((HEADS, span), 0) // G

    def first_keys():
        loads["tk"].wait()
        sort_keys(tk_raw, k_te, 0, positions // 2, 0)

    def last_keys():
        sort_keys(tk_raw, k_te, positions // 2, positions, 0)

    def own_shared():
        loads["sk"].wait()
        sort_keys(sk_raw.at[0], k_sh, 0, half, 0)
        loads["sv"].wait()
        sort_values(sv_raw.at[0], v_sh, 0, half, 0)

    def first_values():
        loads["tv"].wait()
        sort_values(tv_raw, v_te, 0, positions // 2, 0)

    def last_values():
        sort_values(tv_raw, v_te, positions // 2, positions, 0)

    work = [
        lambda: (mark(0), mark(1)),
        lambda: (mark(2), mark(3)),
        first_keys,
        last_keys,
        own_shared,
        first_values,
        last_values,
    ]
    last = len(groups) - 1
    for turn in range(max(len(work), last + 3)):
        if turn < len(work):
            work[turn]()
        if turn < last:
            z_wait(q_all, qz_s, qz_r, turn + 1)
            forward(*q_line, turn + 1)
        if 1 <= turn <= last + 1:
            relay(*q_line, turn - 1)
    loads["pk"].wait()
    loads["pv"].wait()
    for group in range(len(groups)):
        far_wait(*q_line, group)

    def chunk_queries(xx, kv):
        return q_all[xx, :, kv * COLUMNS:(kv + 1) * COLUMNS, :].reshape(zcols, D)

    for kv in range(KV):
        total = dot(onehot[0], chunk_queries(0, kv))
        for xx in range(1, NX):
            total += dot(onehot[xx], chunk_queries(xx, kv))
        qt_send[kv] = total.astype(BF16)
    go(qt_send, qt_recv, pair_s.at[2], pair_r.at[2], pair)

    arrived(sk_raw.at[1], pair_s.at[0], pair_r.at[0])
    sort_keys(sk_raw.at[1], k_sh, 0, half, half)
    arrived(sv_raw.at[1], pair_s.at[1], pair_r.at[1])
    sort_values(sv_raw.at[1], v_sh, 0, half, half)

    width = min(256, zcols)

    def shared(xx):
        for kv in range(KV):
            for c in range(0, zcols, width):
                zs = slice(c // COLUMNS, (c + width) // COLUMNS)
                queries = q_all[xx, zs, kv * COLUMNS:(kv + 1) * COLUMNS, :].reshape(width, D)
                s = dot_t(k_sh[kv], queries)
                m = jnp.max(s, axis=0, keepdims=True)
                p = jnp.exp2((s - m) * SCALE)
                l = jnp.sum(p, axis=0, keepdims=True)
                sh_o[xx, kv, :, c:c + width] = dot(v_sh[kv], p.astype(BF16)) / l
                lse = m * SCALE + jnp.log2(l)
                sh_l[xx, kv, :, c:c + width] = jnp.broadcast_to(lse, (8, width))

    for r in range(R // 2):
        private(r)
    shared(3)

    arrived(qt_recv, pair_s.at[2], pair_r.at[2])
    extent = tlen_ref[tenant] - lax.rem(seq, 4) * positions
    step_size = min(1024, positions)
    for kv in range(KV):
        queries = (qt_send[kv].astype(F32) + qt_recv[kv].astype(F32)).astype(BF16)
        te_m[...] = jnp.full(te_m.shape, DEAD, F32)
        te_l[...] = jnp.zeros(te_l.shape, F32)
        te_acc[...] = jnp.zeros(te_acc.shape, F32)

        def step(i, carry):
            base = pl.multiple_of(i * step_size, step_size)
            s = dot_t(k_te[kv, pl.ds(base, step_size), :], queries)
            s = jnp.where(iota((step_size, SLOTS), 0) < extent - base, s, DEAD)
            m_old = te_m[:1]
            m = jnp.maximum(m_old, jnp.max(s, axis=0, keepdims=True))
            p = jnp.exp2((s - m) * SCALE)
            keep = jnp.exp2((m_old - m) * SCALE)
            te_m[:1] = m
            te_l[:1] = te_l[:1] * keep + jnp.sum(p, axis=0, keepdims=True)
            te_acc[...] = te_acc[...] * keep + dot(v_te[kv, :, pl.ds(base, step_size)], p.astype(BF16))
            return carry

        lax.fori_loop(0, positions // step_size, step, 0)
        l = te_l[:1]
        to_send[kv] = (te_acc[...] / l).astype(BF16)
        lse = jnp.where(extent > 0, te_m[:1] * SCALE + jnp.log2(l), DEAD)
        tl_send[kv] = jnp.broadcast_to(lse, (8, SLOTS))
    go(to_send, to_recv, pair_s.at[3], pair_r.at[3], pair)
    go(tl_send, tl_recv, pair_s.at[4], pair_r.at[4], pair)
    go(w_hbm, w.at[1], pair_s.at[5], pair_r.at[5], pair)

    def tenants():
        arrived(to_recv, pair_s.at[3], pair_r.at[3])
        arrived(tl_recv, pair_s.at[4], pair_r.at[4])
        for kv in range(KV):
            l1, l2 = tl_send[kv][:1], tl_recv[kv][:1]
            top = jnp.maximum(l1, l2)
            w1, w2 = jnp.exp2(l1 - top), jnp.exp2(l2 - top)
            whole = w1 + w2
            o = to_send[kv].astype(F32) * (w1 / whole) + to_recv[kv].astype(F32) * (w2 / whole)
            hi = o.astype(BF16)
            te_hi[kv] = hi
            te_lo[kv] = (o - hi.astype(F32)).astype(BF16)
            te_stat[kv] = split3(top + jnp.log2(whole))

    near = zcols // 2

    def merge(slot, extra=None):
        for kv in range(KV):
            for side in range(2):
                cut = slice(side * near, (side + 1) * near)
                spread = onehot[slot, :, cut]
                lse = join3(dot(te_stat[kv], spread))
                lse = jnp.where(keys[slot, :1, cut] >= 0.0, lse, DEAD)
                pieces = [
                    (sh_l[slot, kv, :1, cut], lambda: sh_o[slot, kv, :, cut]),
                    (lse, lambda: dot(te_hi[kv], spread) + dot(te_lo[kv], spread)),
                ]
                if extra == side:
                    pieces.append((join3(xo_half[side, kv, D:, :]), lambda: xo_half[side, kv, :D, :]))
                o, lse = combine(pieces)
                if slot == 0:
                    sh_o[0, kv, :, cut] = o
                    sh_l[0, kv, :, cut] = jnp.broadcast_to(lse, (8, near))
                else:
                    xo_send[slot - 1, kv, :D, cut] = o.astype(BF16)
                    xo_send[slot - 1, kv, D:, cut] = split3(lse)

    for r in range(R // 2, R):
        private(r)
    shared(1)
    shared(2)
    tenants()
    merge(3)
    go(xo_send.at[2, :, :, pl.ds(0, near)], xo_half.at[0], xo_s.at[0], xo_r.at[0], right)
    go(xo_send.at[2, :, :, pl.ds(near, near)], xo_half.at[1], xo_s.at[1], xo_r.at[1], left)
    shared(0)
    merge(0)
    arrived(xo_half.at[0], xo_s.at[0], xo_r.at[0])
    merge(1, 0)
    go(xo_send.at[0], xo_full.at[0], xo_s.at[2], xo_r.at[2], right)
    arrived(xo_half.at[1], xo_s.at[1], xo_r.at[1])
    merge(2, 1)
    go(xo_send.at[1], xo_full.at[1], xo_s.at[3], xo_r.at[3], left)
    arrived(xo_full.at[0], xo_s.at[2], xo_r.at[2])
    arrived(xo_full.at[1], xo_s.at[3], xo_r.at[3])

    both = 2 * COLUMNS
    low = iota((D, both), 1) < COLUMNS
    for c in range(0, zcols, both):
        cut = slice(c, c + both)
        halves, marks = [], []
        for kv in range(KV):
            pieces = [(sh_l[0, kv, :1, cut], lambda: sh_o[0, kv, :, cut])]
            for side in range(2):
                pieces.append((
                    join3(xo_full[side, kv, D:, cut]),
                    lambda side=side: xo_full[side, kv, :D, cut],
                ))
            o, lse = combine(pieces)
            halves.append(o)
            marks.append(jnp.broadcast_to(lse, (8, both)))
        first_o = jnp.where(low, halves[0], pltpu.roll(halves[1], COLUMNS, 1))
        first_l = jnp.where(low[:8], marks[0], pltpu.roll(marks[1], COLUMNS, 1))
        second_o = jnp.where(low, pltpu.roll(halves[0], COLUMNS, 1), halves[1])
        second_l = jnp.where(low[:8], pltpu.roll(marks[0], COLUMNS, 1), marks[1])
        for p, o, lse in ((c // COLUMNS, first_o, first_l), (c // COLUMNS + 1, second_o, second_l)):
            if p == 0:
                zo_own[...] = o
                zl_own[...] = lse
            else:
                q = back(p)
                zo_send[p - 1, :D] = o.astype(BF16)
                zo_send[p - 1, D:] = split3(lse[:1])
                to = device(z_of(zorder[p]), x, b, h)
                go(zo_send.at[p - 1], zo_recv.at[q - 1], zo_s.at[p - 1], zo_r.at[q - 1], to)

    private_o = pr_o[...].T
    private_l = pr_l[...].T[:1]
    pieces = [(private_l, lambda: private_o), (zl_own[:1], lambda: zo_own[...])]
    for p in range(1, NZ):
        arrived(zo_recv.at[p - 1], zo_s.at[p - 1], zo_r.at[p - 1])
        pieces.append((join3(zo_recv[p - 1, D:]), lambda p=p: zo_recv[p - 1, :D]))
    attended, _ = combine(pieces)
    at[0, 0] = attended.T.astype(BF16)

    at_line = (at, ax_s, ax_r)
    z_start(at, az_s, az_r)
    forward(*at_line, 0)
    for group in range(1, len(groups)):
        z_wait(at, az_s, az_r, group)
        forward(*at_line, group)
        relay(*at_line, group - 1)
    relay(*at_line, len(groups) - 1)

    def project(slot):
        wide = at[slot].astype(F32)
        rows = [
            wide[:, i * R:(i + 1) * R, :].reshape(NZ * R, D).astype(BF16) for i in range(HEADS)
        ]
        rows = jnp.concatenate(rows, axis=1)
        for db in range(2):
            sums = dot(rows, w[db])
            for p in range(NZ):
                part[db, z_of(zorder[p]), x_of(xorder[slot])] = sums[p * R:(p + 1) * R]

    loads["w"].wait()
    arrived(w.at[1], pair_s.at[5], pair_r.at[5])
    for slot in range(3):
        project(slot)
    for group in range(len(groups)):
        far_wait(*at_line, group)
    project(3)

    for k in range(1, 2 * NH):
        dh, db = k // 2, k % 2
        src = part.at[db, pl.ds(h_of(dh) * zper, zper)]
        go(src, rs_recv.at[k - 1], rs_s.at[k - 1], rs_r.at[k - 1], device(z, x, b_of(db), h_of(dh)))
    totals = [part[0, pl.ds(h * zper, zper)], None]
    for k in range(1, 2 * NH):
        arrived(rs_recv.at[k - 1], rs_s.at[k - 1], rs_r.at[k - 1])
        got = rs_recv[k - 1]
        totals[k % 2] = got if totals[k % 2] is None else totals[k % 2] + got
    first = jnp.where(b == 0, totals[0], totals[1])
    second = jnp.where(b == 0, totals[1], totals[0])
    rows = jnp.concatenate([first[:, :, None], second[:, :, None]], axis=2)
    out_ref[...] = rows.reshape(zper * NX * 2 * R, D).astype(BF16)

    for copy in started:
        copy.wait_send()


def local(NZ, NX, NH, queries, sk, sv, tk, tv, ids, tlen, plen, ptab, pk, pv, w):
    flat = lambda rows: rows.reshape(rows.shape[0] * KV, D)
    paged = lambda rows: rows.reshape(rows.shape[0], rows.shape[1] * KV, D)
    sk, sv, tk, tv = flat(sk), flat(sv), flat(tk), flat(tv)
    pk, pv = paged(pk), paged(pv)
    shared2, positions = sk.shape[0], tk.shape[0] // KV
    zcols = NZ * COLUMNS
    zper = NZ // NH
    dma = pltpu.SemaphoreType.DMA
    v = pltpu.VMEM
    scratch = [
        v(queries.shape, BF16), v((R * HEADS, D), F32),
        v((2, shared2, D), BF16), v((2, shared2, D), BF16), v(tk.shape, BF16), v(tv.shape, BF16),
        v(pk.shape, BF16), v(pv.shape, BF16), v((2,) + w.shape, BF16),
        v((KV, shared2, D), BF16), v((KV, D, shared2), BF16),
        v((KV, positions, D), BF16), v((KV, D, positions), BF16),
        v((NX, NZ, R * HEADS, D), BF16), v((NX, SLOTS, zcols), BF16), v((NX, 8, zcols), F32),
        v((KV, SLOTS, D), BF16), v((KV, SLOTS, D), BF16),
        v((8, SLOTS), F32), v((8, SLOTS), F32), v((D, SLOTS), F32),
        v((KV, D, SLOTS), BF16), v((KV, D, SLOTS), BF16),
        v((KV, 8, SLOTS), F32), v((KV, 8, SLOTS), F32),
        v((KV, D, SLOTS), BF16), v((KV, D, SLOTS), BF16), v((KV, 16, SLOTS), BF16),
        v((NX, KV, D, zcols), F32), v((NX, KV, 8, zcols), F32),
        v((3, KV, D + STAT, zcols), BF16), v((2, KV, D + STAT, zcols // 2), BF16),
        v((2, KV, D + STAT, zcols), BF16),
        v((D, R * HEADS), F32), v((8, R * HEADS), F32),
        v((NZ - 1, D + STAT, R * HEADS), BF16), v((NZ - 1, D + STAT, R * HEADS), BF16),
        v((R * HEADS, D), F32), v((R * HEADS, D), F32),
        v((NX, NZ, R * HEADS, D), BF16), v((2, NZ, NX, R, D), F32),
        v((2 * NH - 1, zper, NX, R, D), F32),
        dma((8,)),
    ]
    lines = 16
    for count in (NZ - 1, lines, 6, 4, NZ - 1, NZ - 1, lines, 2 * NH - 1):
        scratch += [dma((count,)), dma((count,))]
    hbm = pl.BlockSpec(memory_space=pl.ANY)
    smem = pl.BlockSpec(memory_space=pltpu.SMEM)
    vmem = pl.BlockSpec(memory_space=pltpu.VMEM)
    return pl.pallas_call(
        functools.partial(kernel, NZ, NX, NH),
        out_shape=jax.ShapeDtypeStruct((zper * NX * 2 * R, D), BF16),
        in_specs=[hbm] * 5 + [vmem, smem, smem, smem] + [hbm] * 3,
        out_specs=vmem,
        scratch_shapes=scratch,
        compiler_params=pltpu.CompilerParams(
            collective_id=0, has_side_effects=True, vmem_limit_bytes=56 * 1024 * 1024
        ),
    )(queries, sk, sv, tk, tv, ids.reshape(1, -1), tlen, plen, ptab, pk, pv, w)


def solution(mesh):
    sizes = dict(mesh.shape)
    NX = 4
    NZ = sizes["seq"] // (2 * NX)
    placed = (
        P("seq", "head", None),
        P("seq", "head", None),
        P("seq", "head", None),
        P("seq", "head", None),
        P("seq", "head", None),
        P(),
        P(),
        P("seq"),
        P("seq", None),
        P("seq", None, "head", None),
        P("seq", None, "head", None),
        P("head", "seq"),
    )
    return jax.shard_map(
        functools.partial(local, NZ, NX, sizes["head"]),
        mesh=mesh, in_specs=placed, out_specs=P("head", "seq"), check_vma=False,
    )
```

```python
import functools
import math

import jax
import jax.numpy as jnp
from jax import lax
from jax.experimental import pallas as pl
from jax.experimental.pallas import tpu as pltpu
from jax.sharding import PartitionSpec as P

MESH = pl.DeviceIdType.MESH
F32 = jnp.float32
BF16 = jnp.bfloat16
DEAD = -1e30
KV = 2
G = 8
D = 128
R = 8
HEADS = KV * G
STAT = 16
CAP = 48
SLOTS = CAP * G
COLUMNS = R * G
LOG2E = math.log2(math.e)
SCALE = LOG2E / math.sqrt(D)


def dot(a, b):
    return jnp.dot(a, b, preferred_element_type=F32)


def dot_t(a, b):
    return lax.dot_general(a, b, (((1,), (1,)), ((), ())), preferred_element_type=F32)


def split3(v):
    terms = []
    for _ in range(3):
        term = v.astype(BF16).astype(F32)
        terms.append(term)
        v = v - term
    terms.append(jnp.zeros((STAT - 3, v.shape[1]), F32))
    return jnp.concatenate(terms, axis=0).astype(BF16)


def join3(rows):
    rows = rows.astype(F32)
    return rows[0:1] + rows[1:2] + rows[2:3]


def combine(pieces):
    top = pieces[0][0]
    for lse, _ in pieces[1:]:
        top = jnp.maximum(top, lse)
    weights = [jnp.exp2(lse - top) for lse, _ in pieces]
    whole = functools.reduce(lambda one, two: one + two, weights)
    inverse = 1.0 / whole
    total = None
    for weight, (_, o) in zip(weights, pieces):
        term = o().astype(F32) * (weight * inverse)
        total = term if total is None else total + term
    return total, top + jnp.log2(whole)


def iota(shape, axis):
    return lax.broadcasted_iota(jnp.int32, shape, axis)


def kernel(
    NZ, NX, NH,
    q_hbm, sk_hbm, sv_hbm, tk_hbm, tv_hbm, ids_ref, tlen_ref, plen_ref, ptab_ref,
    pk_hbm, pv_hbm, w_hbm, out_ref,
    q_raw, q_wide, sk_raw, sv_raw, tk_raw, tv_raw, pk, pv, w,
    k_sh, v_sh, k_te, v_te,
    q_all, onehot, keys, qt_send, qt_recv,
    te_m, te_l, te_acc, te_own, te_lse, to_send, to_recv,
    te_hi, te_lo, te_stat, sh_o, sh_l,
    xo_send, xo_half, xo_full, zo_own, zl_own, zo_send, zo_recv,
    pr_o, pr_l, at, part, rs_recv, fx_send, final,
    in_sem,
    qz_s, qz_r, qx_s, qx_r, pair_s, pair_r, xo_s, xo_r,
    zo_s, zo_r, az_s, az_r, wx_s, wx_r, rs_s, rs_r, fx_s, fx_r,
):
    seq = lax.axis_index("seq")
    h = lax.axis_index("head")
    b = lax.rem(seq, 2)
    x = lax.rem(seq // 2, NX)
    z = seq // (2 * NX)
    pages = pk.shape[0]
    zcols = NZ * COLUMNS
    zper = NZ // NH

    def seq_of(zz, xx, bb):
        return (zz * NX + xx) * 2 + bb

    def device(zz, xx, bb, hh):
        return {"seq": seq_of(zz, xx, bb), "head": hh}

    zorder = [(p + 1) // 2 if p % 2 else -(p // 2) for p in range(NZ)]
    xorder = [0, 1, -1, 2]
    cuts = [0, 1, 5, 8] if NZ == 8 else [0, 1, NZ]
    groups = list(zip(cuts[:-1], cuts[1:]))

    def back(p):
        return [(zorder[p] + other) % NZ for other in zorder].index(0)

    def z_of(dz):
        return lax.rem(z + dz + NZ, NZ)

    def x_of(dx):
        return lax.rem(x + dx + NX, NX)

    def h_of(dh):
        return lax.rem(h + dh + NH, NH)

    def b_of(db):
        return lax.rem(b + db, 2)

    def send(src, dst, s, r, dev):
        return pltpu.make_async_remote_copy(
            src_ref=src, dst_ref=dst, send_sem=s, recv_sem=r, device_id=dev, device_id_type=MESH
        )

    me = device(z, x, b, h)
    pair = device(z, x, b_of(1), h)
    started = []

    def go(*args):
        copy = send(*args)
        copy.start()
        started.append(copy)

    def arrived(ref, s, r):
        send(ref, ref, s, r, pair).wait_recv()

    loads = {}
    for at_sem, (name, src, dst) in enumerate((
        ("q", q_hbm, q_raw),
        ("tk", tk_hbm, tk_raw),
        ("sk", sk_hbm, sk_raw.at[0]),
        ("sv", sv_hbm, sv_raw.at[0]),
        ("tv", tv_hbm, tv_raw),
        ("pk", pk_hbm, pk),
        ("pv", pv_hbm, pv),
        ("w", w_hbm, w.at[0, 0]),
    )):
        loads[name] = pltpu.make_async_copy(src, dst, in_sem.at[at_sem])
        loads[name].start()

    barrier = pltpu.get_barrier_semaphore()
    peers = [device(z_of(dz), x, b, h) for dz in range(1, NZ)]
    peers += [device(z, x_of(dx), b, h) for dx in range(1, NX)]
    peers += [
        device(z, x, b_of(db), h_of(dh)) for dh in range(NH) for db in range(2) if dh + db > 0
    ]
    for peer in peers:
        pl.semaphore_signal(barrier, inc=1, device_id=peer, device_id_type=MESH)

    loads["q"].wait()
    q_wide[...] = q_raw[...].astype(F32).reshape(R * HEADS, D)
    q_all[0, 0] = jnp.concatenate(
        [q_wide[pl.ds(i, R, stride=HEADS), :] for i in range(HEADS)], axis=0
    ).astype(BF16)

    pl.semaphore_wait(barrier, len(peers))

    left, right, far = device(z, x_of(-1), b, h), device(z, x_of(1), b, h), device(z, x_of(2), b, h)

    def z_start(buf, zs, zr):
        for p in range(1, NZ):
            q = back(p)
            go(buf.at[0, 0], buf.at[0, q], zs.at[p - 1], zr.at[q - 1], device(z_of(zorder[p]), x, b, h))

    def z_wait(buf, zs, zr, group):
        for p in range(*groups[group]):
            if p > 0:
                arrived(buf.at[0, p], zs.at[p - 1], zr.at[p - 1])

    def block(slot, group):
        first, last = groups[group]
        return q_all.at[slot, pl.ds(first, last - first)]

    def forward(group):
        for slot, to in ((2, right), (1, left), (3, far)):
            k = 3 * group + slot - 1
            go(block(0, group), block(slot, group), qx_s.at[k], qx_r.at[k], to)

    def x_wait(slot):
        for group in range(len(groups)):
            k = 3 * group + slot - 1
            arrived(block(slot, group), qx_s.at[k], qx_r.at[k])

    z_start(q_all, qz_s, qz_r)
    forward(0)
    go(sk_hbm, sk_raw.at[1], pair_s.at[0], pair_r.at[0], pair)
    go(sv_hbm, sv_raw.at[1], pair_s.at[1], pair_r.at[1], pair)
    go(w_hbm, w.at[0, 1], pair_s.at[2], pair_r.at[2], pair)

    row, col = iota((2 * D, 2 * D), 0), iota((2 * D, 2 * D), 1)
    sort = (col == jnp.where(row < D, 2 * row, 2 * (row - D) + 1)).astype(F32).astype(BF16)

    def sort_keys(raw, into, first, last, base):
        def step(i, carry):
            at_row = pl.multiple_of(i * 2 * D, 2 * D)
            to_row = pl.multiple_of(base + i * D, D)
            rows = dot(sort, raw[pl.ds(at_row, 2 * D), :]).astype(BF16)
            into[0, pl.ds(to_row, D), :] = rows[:D]
            into[1, pl.ds(to_row, D), :] = rows[D:]
            return carry

        lax.fori_loop(first // D, last // D, step, 0, unroll=4)

    def sort_values(raw, into, first, last, base):
        def step(i, carry):
            at_row = pl.multiple_of(i * 2 * D, 2 * D)
            to_row = pl.multiple_of(base + i * D, D)
            rows = dot(sort, raw[pl.ds(at_row, 2 * D), :])
            into[0, :, pl.ds(to_row, D)] = rows[:D].T.astype(BF16)
            into[1, :, pl.ds(to_row, D)] = rows[D:].T.astype(BF16)
            return carry

        lax.fori_loop(first // D, last // D, step, 0, unroll=4)

    positions = k_te.shape[1]
    half = sk_raw.shape[1] // 2

    tenant = seq // 4
    requests = ids_ref.shape[1]
    match = (ids_ref[...] == tenant).astype(F32)
    match = jnp.broadcast_to(match, (16, requests))
    upto = (iota((requests, requests), 0) <= iota((requests, requests), 1)).astype(F32).astype(BF16)
    slot = (match * dot(match.astype(BF16), upto)).astype(BF16)

    def mark(xx):
        j = iota((1, zcols), 1)
        place = j // COLUMNS
        away = jnp.where(place % 2 == 1, (place + 1) // 2, -(place // 2))
        owner = seq_of(lax.rem(z + away + NZ, NZ), x_of(xorder[xx]), b)
        request = owner * R + lax.rem(j, R)
        pick = (iota((requests, zcols), 0) == request).astype(F32).astype(BF16)
        found = dot(slot, pick)[:1]
        group = (lax.rem(j, COLUMNS) // R).astype(F32)
        key = jnp.where(found > 0.5, group * CAP + found - 1.0, -1.0)
        keys[xx] = jnp.broadcast_to(key, (8, zcols))
        onehot[xx] = (iota((SLOTS, zcols), 0).astype(F32) == key).astype(F32).astype(BF16)

    def private(r):
        keys_here = jnp.concatenate([pk[ptab_ref[r, p]] for p in range(ptab_ref.shape[1])], axis=0)
        values_here = jnp.concatenate([pv[ptab_ref[r, p]] for p in range(ptab_ref.shape[1])], axis=0)
        s = dot_t(q_raw[r], keys_here)
        s = jnp.where(own & (lane // 2 < plen_ref[r]), s, DEAD)
        m = jnp.max(s, axis=1, keepdims=True)
        p = jnp.exp2((s - m) * SCALE)
        l = jnp.sum(p, axis=1, keepdims=True)
        o = dot(p.astype(BF16), values_here) / l
        lse = jnp.where(plen_ref[r] > 0, m * SCALE + jnp.log2(l), DEAD)
        pr_o[pl.ds(r, HEADS, stride=R), :] = o
        pr_l[pl.ds(r, HEADS, stride=R), :] = jnp.broadcast_to(lse, (HEADS, D))

    span = ptab_ref.shape[1] * pk.shape[1]
    lane = iota((HEADS, span), 1)
    own = lax.rem(lane, 2) == iota((HEADS, span), 0) // G

    def first_keys():
        loads["tk"].wait()
        sort_keys(tk_raw, k_te, 0, positions // 2, 0)

    def last_keys():
        sort_keys(tk_raw, k_te, positions // 2, positions, 0)

    def own_shared():
        loads["sk"].wait()
        sort_keys(sk_raw.at[0], k_sh, 0, half, 0)
        loads["sv"].wait()
        sort_values(sv_raw.at[0], v_sh, 0, half, 0)

    def first_values():
        loads["tv"].wait()
        sort_values(tv_raw, v_te, 0, positions // 2, 0)

    def last_values():
        sort_values(tv_raw, v_te, positions // 2, positions, 0)

    def pair_shared():
        arrived(sk_raw.at[1], pair_s.at[0], pair_r.at[0])
        sort_keys(sk_raw.at[1], k_sh, 0, half, half)
        arrived(sv_raw.at[1], pair_s.at[1], pair_r.at[1])
        sort_values(sv_raw.at[1], v_sh, 0, half, half)

    width = min(256, zcols)

    def shared(xx):
        for kv in range(KV):
            for c in range(0, zcols, width):
                zs = slice(c // COLUMNS, (c + width) // COLUMNS)
                queries = q_all[xx, zs, kv * COLUMNS:(kv + 1) * COLUMNS, :].reshape(width, D)
                s = dot_t(k_sh[kv], queries)
                m = jnp.max(s, axis=0, keepdims=True)
                p = jnp.exp2((s - m) * SCALE)
                l = jnp.sum(p, axis=0, keepdims=True)
                sh_o[xx, kv, :, c:c + width] = dot(v_sh[kv], p.astype(BF16)) / l
                lse = m * SCALE + jnp.log2(l)
                sh_l[xx, kv, :, c:c + width] = jnp.broadcast_to(lse, (8, width))

    mark(0)
    mark(1)
    z_wait(q_all, qz_s, qz_r, 1)
    forward(1)
    mark(2)
    mark(3)
    for group in range(2, len(groups)):
        z_wait(q_all, qz_s, qz_r, group)
        forward(group)
    first_keys()
    last_keys()
    own_shared()
    loads["pk"].wait()
    loads["pv"].wait()
    for r in range(R):
        private(r)
    pair_shared()
    shared(0)
    first_values()
    for slot_at in (2, 1, 3):
        x_wait(slot_at)

    def chunk_queries(xx, kv):
        return q_all[xx, :, kv * COLUMNS:(kv + 1) * COLUMNS, :].reshape(zcols, D)

    for kv in range(KV):
        total = dot(onehot[0], chunk_queries(0, kv))
        for xx in range(1, NX):
            total += dot(onehot[xx], chunk_queries(xx, kv))
        qt_send[kv] = total.astype(BF16)
        go(qt_send.at[kv], qt_recv.at[kv], pair_s.at[3 + kv], pair_r.at[3 + kv], pair)

    last_values()
    loads["w"].wait()
    arrived(w.at[0, 1], pair_s.at[2], pair_r.at[2])
    go(w.at[0], w.at[2], wx_s.at[0], wx_r.at[0], right)
    go(w.at[0], w.at[1], wx_s.at[1], wx_r.at[1], left)
    shared(1)
    shared(2)

    extent = tlen_ref[tenant] - lax.rem(seq, 4) * positions
    step_size = min(1024, positions)

    def tenant_part(kv):
        arrived(qt_recv.at[kv], pair_s.at[3 + kv], pair_r.at[3 + kv])
        queries = (qt_send[kv].astype(F32) + qt_recv[kv].astype(F32)).astype(BF16)
        te_m[...] = jnp.full(te_m.shape, DEAD, F32)
        te_l[...] = jnp.zeros(te_l.shape, F32)
        te_acc[...] = jnp.zeros(te_acc.shape, F32)

        def step(i, carry):
            base = pl.multiple_of(i * step_size, step_size)
            s = dot_t(k_te[kv, pl.ds(base, step_size), :], queries)
            s = jnp.where(iota((step_size, SLOTS), 0) < extent - base, s, DEAD)
            m_old = te_m[:1]
            m = jnp.maximum(m_old, jnp.max(s, axis=0, keepdims=True))
            p = jnp.exp2((s - m) * SCALE)
            keep = jnp.exp2((m_old - m) * SCALE)
            te_m[:1] = m
            te_l[:1] = te_l[:1] * keep + jnp.sum(p, axis=0, keepdims=True)
            te_acc[...] = te_acc[...] * keep + dot(v_te[kv, :, pl.ds(base, step_size)], p.astype(BF16))
            return carry

        lax.fori_loop(0, positions // step_size, step, 0)
        l = te_l[:1]
        o = te_acc[...] * (1.0 / l)
        lse = jnp.where(extent > 0, te_m[:1] * SCALE + jnp.log2(l), DEAD)
        te_own[kv] = o
        te_lse[kv] = jnp.broadcast_to(lse, (8, SLOTS))
        to_send[kv, :D] = o.astype(BF16)
        to_send[kv, D:] = split3(lse)
        go(to_send.at[kv], to_recv.at[kv], pair_s.at[5 + kv], pair_r.at[5 + kv], pair)

    def tenants(kv):
        arrived(to_recv.at[kv], pair_s.at[5 + kv], pair_r.at[5 + kv])
        o, lse = combine([
            (te_lse[kv, :1], lambda: te_own[kv]),
            (join3(to_recv[kv, D:]), lambda: to_recv[kv, :D]),
        ])
        hi = o.astype(BF16)
        te_hi[kv] = hi
        te_lo[kv] = (o - hi.astype(F32)).astype(BF16)
        te_stat[kv] = split3(lse)

    tenant_part(0)
    tenant_part(1)
    shared(3)

    near = zcols // 2

    def merge(slot, kv, extra=None):
        for side in range(2):
            cut = slice(side * near, (side + 1) * near)
            spread = onehot[slot, :, cut]
            lse = join3(dot(te_stat[kv], spread))
            lse = jnp.where(keys[slot, :1, cut] >= 0.0, lse, DEAD)
            pieces = [
                (sh_l[slot, kv, :1, cut], lambda: sh_o[slot, kv, :, cut]),
                (lse, lambda: dot(te_hi[kv], spread) + dot(te_lo[kv], spread)),
            ]
            if extra == side:
                pieces.append((join3(xo_half[side, kv, D:, :]), lambda: xo_half[side, kv, :D, :]))
            o, lse = combine(pieces)
            if slot == 0:
                sh_o[0, kv, :, cut] = o
                sh_l[0, kv, :, cut] = jnp.broadcast_to(lse, (8, near))
            else:
                xo_send[slot - 1, kv, :D, cut] = o.astype(BF16)
                xo_send[slot - 1, kv, D:, cut] = split3(lse)

    for kv in range(KV):
        tenants(kv)
        merge(3, kv)
        for side, to in ((0, right), (1, left)):
            k = 4 * kv + side
            half_cut = pl.ds(side * near, near)
            go(xo_send.at[2, kv, :, half_cut], xo_half.at[side, kv], xo_s.at[k], xo_r.at[k], to)
    for kv in range(KV):
        merge(0, kv)
    for kv in range(KV):
        for side, to in ((0, right), (1, left)):
            k = 4 * kv + side
            arrived(xo_half.at[side, kv], xo_s.at[k], xo_r.at[k])
            merge(1 + side, kv, side)
            go(xo_send.at[side, kv], xo_full.at[side, kv], xo_s.at[k + 2], xo_r.at[k + 2], to)
    private_o = pr_o[...].T
    private_l = pr_l[...].T[:1]
    for kv in range(KV):
        for side in range(2):
            k = 4 * kv + side + 2
            arrived(xo_full.at[side, kv], xo_s.at[k], xo_r.at[k])

    both = 2 * COLUMNS
    low = iota((D, both), 1) < COLUMNS
    for c in range(0, zcols, both):
        cut = slice(c, c + both)
        halves, marks = [], []
        for kv in range(KV):
            pieces = [(sh_l[0, kv, :1, cut], lambda: sh_o[0, kv, :, cut])]
            for side in range(2):
                pieces.append((
                    join3(xo_full[side, kv, D:, cut]),
                    lambda side=side: xo_full[side, kv, :D, cut],
                ))
            o, lse = combine(pieces)
            halves.append(o)
            marks.append(jnp.broadcast_to(lse, (8, both)))
        first_o = jnp.where(low, halves[0], pltpu.roll(halves[1], COLUMNS, 1))
        first_l = jnp.where(low[:8], marks[0], pltpu.roll(marks[1], COLUMNS, 1))
        second_o = jnp.where(low, pltpu.roll(halves[0], COLUMNS, 1), halves[1])
        second_l = jnp.where(low[:8], pltpu.roll(marks[0], COLUMNS, 1), marks[1])
        for p, o, lse in ((c // COLUMNS, first_o, first_l), (c // COLUMNS + 1, second_o, second_l)):
            if p == 0:
                zo_own[...] = o
                zl_own[...] = lse
            else:
                q = back(p)
                zo_send[p - 1, :D] = o.astype(BF16)
                zo_send[p - 1, D:] = split3(lse[:1])
                to = device(z_of(zorder[p]), x, b, h)
                go(zo_send.at[p - 1], zo_recv.at[q - 1], zo_s.at[p - 1], zo_r.at[q - 1], to)

    arrived(w.at[2], wx_s.at[0], wx_r.at[0])
    go(w.at[2, 0], w.at[3, 0], wx_s.at[2], wx_r.at[2], right)
    arrived(w.at[1], wx_s.at[1], wx_r.at[1])
    go(w.at[1, 1], w.at[3, 1], wx_s.at[3], wx_r.at[3], left)

    pieces = [(private_l, lambda: private_o), (zl_own[:1], lambda: zo_own[...])]
    for p in range(1, NZ):
        arrived(zo_recv.at[p - 1], zo_s.at[p - 1], zo_r.at[p - 1])
        pieces.append((join3(zo_recv[p - 1, D:]), lambda p=p: zo_recv[p - 1, :D]))
    attended, _ = combine(pieces)
    at[0, 0] = attended.T.astype(BF16)

    z_start(at, az_s, az_r)
    for group in range(len(groups)):
        z_wait(at, az_s, az_r, group)
    wide = at[0].astype(F32)
    rows = jnp.concatenate([
        wide[:, i * R:(i + 1) * R, :].reshape(NZ * R, D).astype(BF16) for i in range(HEADS)
    ], axis=1)
    arrived(w.at[3, 0], wx_s.at[2], wx_r.at[2])
    arrived(w.at[3, 1], wx_s.at[3], wx_r.at[3])
    for db in (1, 0):
        for slot in range(NX):
            sums = dot(rows, w[slot, db])
            for p in range(NZ):
                part[db, z_of(zorder[p]), slot] = sums[p * R:(p + 1) * R]

    for k in range(1, 2 * NH):
        dh, db = k // 2, k % 2
        src = part.at[db, pl.ds(h_of(dh) * zper, zper)]
        go(src, rs_recv.at[k - 1], rs_s.at[k - 1], rs_r.at[k - 1], device(z, x, b_of(db), h_of(dh)))
    totals = [part[0, pl.ds(h * zper, zper)], None]
    for k in range(1, 2 * NH):
        arrived(rs_recv.at[k - 1], rs_s.at[k - 1], rs_r.at[k - 1])
        got = rs_recv[k - 1]
        totals[k % 2] = got if totals[k % 2] is None else totals[k % 2] + got
    first = jnp.where(b == 0, totals[0], totals[1])
    second = jnp.where(b == 0, totals[1], totals[0])

    for slot, to in ((3, far), (1, right), (2, left), (0, None)):
        rows = jnp.concatenate([first[:, slot], second[:, slot]], axis=1).astype(BF16)
        if to is None:
            final[:, x] = rows
        else:
            fx_send[slot - 1] = rows
            k = slot - 1
            go(fx_send.at[k], final.at[:, x], fx_s.at[k], fx_r.at[k], to)
    for slot, offset in ((3, 2), (1, -1), (2, 1)):
        arrived(final.at[:, x_of(offset)], fx_s.at[slot - 1], fx_r.at[slot - 1])
    out_ref[...] = final[...].reshape(zper * NX * 2 * R, D)

    for copy in started:
        copy.wait_send()


def local(NZ, NX, NH, queries, sk, sv, tk, tv, ids, tlen, plen, ptab, pk, pv, w):
    flat = lambda rows: rows.reshape(rows.shape[0] * KV, D)
    paged = lambda rows: rows.reshape(rows.shape[0], rows.shape[1] * KV, D)
    sk, sv, tk, tv = flat(sk), flat(sv), flat(tk), flat(tv)
    pk, pv = paged(pk), paged(pv)
    shared2, positions = sk.shape[0], tk.shape[0] // KV
    zcols = NZ * COLUMNS
    zper = NZ // NH
    dma = pltpu.SemaphoreType.DMA
    v = pltpu.VMEM
    scratch = [
        v(queries.shape, BF16), v((R * HEADS, D), F32),
        v((2, shared2, D), BF16), v((2, shared2, D), BF16), v(tk.shape, BF16), v(tv.shape, BF16),
        v(pk.shape, BF16), v(pv.shape, BF16), v((NX, 2) + w.shape, BF16),
        v((KV, shared2, D), BF16), v((KV, D, shared2), BF16),
        v((KV, positions, D), BF16), v((KV, D, positions), BF16),
        v((NX, NZ, R * HEADS, D), BF16), v((NX, SLOTS, zcols), BF16), v((NX, 8, zcols), F32),
        v((KV, SLOTS, D), BF16), v((KV, SLOTS, D), BF16),
        v((8, SLOTS), F32), v((8, SLOTS), F32), v((D, SLOTS), F32),
        v((KV, D, SLOTS), F32), v((KV, 8, SLOTS), F32),
        v((KV, D + STAT, SLOTS), BF16), v((KV, D + STAT, SLOTS), BF16),
        v((KV, D, SLOTS), BF16), v((KV, D, SLOTS), BF16), v((KV, 16, SLOTS), BF16),
        v((NX, KV, D, zcols), F32), v((NX, KV, 8, zcols), F32),
        v((3, KV, D + STAT, zcols), BF16), v((2, KV, D + STAT, zcols // 2), BF16),
        v((2, KV, D + STAT, zcols), BF16),
        v((D, R * HEADS), F32), v((8, R * HEADS), F32),
        v((NZ - 1, D + STAT, R * HEADS), BF16), v((NZ - 1, D + STAT, R * HEADS), BF16),
        v((R * HEADS, D), F32), v((R * HEADS, D), F32),
        v((1, NZ, R * HEADS, D), BF16), v((2, NZ, NX, R, D), F32),
        v((2 * NH - 1, zper, NX, R, D), F32),
        v((NX - 1, zper, 2 * R, D), BF16), v((zper, NX, 2 * R, D), BF16),
        dma((8,)),
    ]
    for count in (NZ - 1, 9, 7, 4 * KV, NZ - 1, NZ - 1, 4, 2 * NH - 1, NX - 1):
        scratch += [dma((count,)), dma((count,))]
    hbm = pl.BlockSpec(memory_space=pl.ANY)
    smem = pl.BlockSpec(memory_space=pltpu.SMEM)
    vmem = pl.BlockSpec(memory_space=pltpu.VMEM)
    return pl.pallas_call(
        functools.partial(kernel, NZ, NX, NH),
        out_shape=jax.ShapeDtypeStruct((zper * NX * 2 * R, D), BF16),
        in_specs=[hbm] * 5 + [vmem, smem, smem, smem] + [hbm] * 3,
        out_specs=vmem,
        scratch_shapes=scratch,
        compiler_params=pltpu.CompilerParams(
            collective_id=0, has_side_effects=True, vmem_limit_bytes=56 * 1024 * 1024
        ),
    )(queries, sk, sv, tk, tv, ids.reshape(1, -1), tlen, plen, ptab, pk, pv, w)


def solution(mesh):
    sizes = dict(mesh.shape)
    NX = 4
    NZ = sizes["seq"] // (2 * NX)
    placed = (
        P("seq", "head", None),
        P("seq", "head", None),
        P("seq", "head", None),
        P("seq", "head", None),
        P("seq", "head", None),
        P(),
        P(),
        P("seq"),
        P("seq", None),
        P("seq", None, "head", None),
        P("seq", None, "head", None),
        P("head", "seq"),
    )
    return jax.shard_map(
        functools.partial(local, NZ, NX, sizes["head"]),
        mesh=mesh, in_specs=placed, out_specs=P("head", "seq"), check_vma=False,
    )
```

```python
import functools
import math

import jax
import jax.numpy as jnp
from jax import lax
from jax.experimental import pallas as pl
from jax.experimental.pallas import tpu as pltpu
from jax.sharding import PartitionSpec as P

MESH = pl.DeviceIdType.MESH
F32 = jnp.float32
BF16 = jnp.bfloat16
DEAD = -1e30
KV = 2
G = 8
D = 128
R = 8
HEADS = KV * G
STAT = 16
CAP = 48
SLOTS = CAP * G
COLUMNS = R * G
LOG2E = math.log2(math.e)
SCALE = LOG2E / math.sqrt(D)


def dot(a, b):
    return jnp.dot(a, b, preferred_element_type=F32)


def dot_t(a, b):
    return lax.dot_general(a, b, (((1,), (1,)), ((), ())), preferred_element_type=F32)


def split3(v):
    terms = []
    for _ in range(3):
        term = v.astype(BF16).astype(F32)
        terms.append(term)
        v = v - term
    terms.append(jnp.zeros((STAT - 3, v.shape[1]), F32))
    return jnp.concatenate(terms, axis=0).astype(BF16)


def join3(rows):
    rows = rows.astype(F32)
    return rows[0:1] + rows[1:2] + rows[2:3]


def combine(pieces):
    top = pieces[0][0]
    for lse, _ in pieces[1:]:
        top = jnp.maximum(top, lse)
    weights = [jnp.exp2(lse - top) for lse, _ in pieces]
    whole = functools.reduce(lambda one, two: one + two, weights)
    inverse = 1.0 / whole
    total = None
    for weight, (_, o) in zip(weights, pieces):
        term = o().astype(F32) * (weight * inverse)
        total = term if total is None else total + term
    return total, top + jnp.log2(whole)


def iota(shape, axis):
    return lax.broadcasted_iota(jnp.int32, shape, axis)


def kernel(
    NZ, NX, NH,
    q_hbm, sk_hbm, sv_hbm, tk_hbm, tv_hbm, ids_ref, tlen_ref, plen_ref, ptab_ref,
    pk_hbm, pv_hbm, w_hbm, out_ref,
    q_raw, q_wide, sk_raw, sv_raw, tk_raw, tv_raw, pk, pv, w,
    k_sh, v_sh, k_te, v_te,
    q_all, onehot, keys, qt_send, qt_recv,
    te_m, te_l, te_own, to_send, to_recv,
    te_all, sh_o, sh_l,
    xo_send, xo_half, xo_full, zo_own, zl_own, zo_send, zo_recv,
    pr_o, pr_l, at, part, rs_recv, fx_send, final,
    in_sem,
    qz_s, qz_r, qx_s, qx_r, pair_s, pair_r, xo_s, xo_r,
    zo_s, zo_r, az_s, az_r, wx_s, wx_r, rs_s, rs_r, fx_s, fx_r,
):
    seq = lax.axis_index("seq")
    h = lax.axis_index("head")
    b = lax.rem(seq, 2)
    x = lax.rem(seq // 2, NX)
    z = seq // (2 * NX)
    pages = pk.shape[0]
    zcols = NZ * COLUMNS
    zper = NZ // NH

    def seq_of(zz, xx, bb):
        return (zz * NX + xx) * 2 + bb

    def device(zz, xx, bb, hh):
        return {"seq": seq_of(zz, xx, bb), "head": hh}

    zorder = [(p + 1) // 2 if p % 2 else -(p // 2) for p in range(NZ)]
    xorder = [0, 1, -1, 2]
    cuts = [0, 1, 5, 8] if NZ == 8 else [0, 1, NZ]
    groups = list(zip(cuts[:-1], cuts[1:]))

    def back(p):
        return [(zorder[p] + other) % NZ for other in zorder].index(0)

    def z_of(dz):
        return lax.rem(z + dz + NZ, NZ)

    def x_of(dx):
        return lax.rem(x + dx + NX, NX)

    def h_of(dh):
        return lax.rem(h + dh + NH, NH)

    def b_of(db):
        return lax.rem(b + db, 2)

    def send(src, dst, s, r, dev):
        return pltpu.make_async_remote_copy(
            src_ref=src, dst_ref=dst, send_sem=s, recv_sem=r, device_id=dev, device_id_type=MESH
        )

    me = device(z, x, b, h)
    pair = device(z, x, b_of(1), h)
    started = []

    def go(*args):
        copy = send(*args)
        copy.start()
        started.append(copy)

    def arrived(ref, s, r):
        send(ref, ref, s, r, pair).wait_recv()

    loads = {}
    for at_sem, (name, src, dst) in enumerate((
        ("q", q_hbm, q_raw),
        ("sk", sk_hbm, sk_raw.at[0]),
        ("sv", sv_hbm, sv_raw.at[0]),
        ("tk", tk_hbm, tk_raw),
        ("tv", tv_hbm, tv_raw),
        ("pk", pk_hbm, pk),
        ("pv", pv_hbm, pv),
        ("w", w_hbm, w.at[0, 0]),
    )):
        loads[name] = pltpu.make_async_copy(src, dst, in_sem.at[at_sem])
        loads[name].start()

    barrier = pltpu.get_barrier_semaphore()
    peers = [device(z_of(dz), x, b, h) for dz in range(1, NZ)]
    peers += [device(z, x_of(dx), b, h) for dx in range(1, NX)]
    peers += [
        device(z, x, b_of(db), h_of(dh)) for dh in range(NH) for db in range(2) if dh + db > 0
    ]
    for peer in peers:
        pl.semaphore_signal(barrier, inc=1, device_id=peer, device_id_type=MESH)

    loads["q"].wait()
    q_wide[...] = q_raw[...].astype(F32).reshape(R * HEADS, D)
    q_all[0, 0] = jnp.concatenate(
        [q_wide[pl.ds(i, R, stride=HEADS), :] for i in range(HEADS)], axis=0
    ).astype(BF16)

    pl.semaphore_wait(barrier, len(peers))

    left, right, far = device(z, x_of(-1), b, h), device(z, x_of(1), b, h), device(z, x_of(2), b, h)

    def z_start(buf, zs, zr):
        for p in range(1, NZ):
            q = back(p)
            go(buf.at[0, 0], buf.at[0, q], zs.at[p - 1], zr.at[q - 1], device(z_of(zorder[p]), x, b, h))

    def z_wait(buf, zs, zr, group):
        for p in range(*groups[group]):
            if p > 0:
                arrived(buf.at[0, p], zs.at[p - 1], zr.at[p - 1])

    def block(slot, group):
        first, last = groups[group]
        return q_all.at[slot, pl.ds(first, last - first)]

    def forward(group):
        for slot, to in ((2, right), (1, left), (3, far)):
            k = 3 * group + slot - 1
            go(block(0, group), block(slot, group), qx_s.at[k], qx_r.at[k], to)

    def x_wait(slot):
        for group in range(len(groups)):
            k = 3 * group + slot - 1
            arrived(block(slot, group), qx_s.at[k], qx_r.at[k])

    z_start(q_all, qz_s, qz_r)
    forward(0)
    loads["sk"].wait()
    go(sk_raw.at[0], sk_raw.at[1], pair_s.at[0], pair_r.at[0], pair)
    loads["sv"].wait()
    go(sv_raw.at[0], sv_raw.at[1], pair_s.at[1], pair_r.at[1], pair)

    row, col = iota((2 * D, 2 * D), 0), iota((2 * D, 2 * D), 1)
    sort = (col == jnp.where(row < D, 2 * row, 2 * (row - D) + 1)).astype(F32).astype(BF16)

    def sort_keys(raw, into, first, last, base):
        def step(i, carry):
            at_row = pl.multiple_of(i * 2 * D, 2 * D)
            to_row = pl.multiple_of(base + i * D, D)
            rows = dot(sort, raw[pl.ds(at_row, 2 * D), :]).astype(BF16)
            into[0, pl.ds(to_row, D), :] = rows[:D]
            into[1, pl.ds(to_row, D), :] = rows[D:]
            return carry

        lax.fori_loop(first // D, last // D, step, 0, unroll=4)

    def sort_values(raw, into, first, last, base):
        def step(i, carry):
            at_row = pl.multiple_of(i * 2 * D, 2 * D)
            to_row = pl.multiple_of(base + i * D, D)
            rows = dot(sort, raw[pl.ds(at_row, 2 * D), :])
            into[0, :, pl.ds(to_row, D)] = rows[:D].T.astype(BF16)
            into[1, :, pl.ds(to_row, D)] = rows[D:].T.astype(BF16)
            return carry

        lax.fori_loop(first // D, last // D, step, 0, unroll=4)

    positions = k_te.shape[1]
    half = sk_raw.shape[1] // 2

    tenant = seq // 4
    requests = ids_ref.shape[1]
    match = (ids_ref[...] == tenant).astype(F32)
    match = jnp.broadcast_to(match, (16, requests))
    upto = (iota((requests, requests), 0) <= iota((requests, requests), 1)).astype(F32).astype(BF16)
    slot = (match * dot(match.astype(BF16), upto)).astype(BF16)

    def mark(xx):
        j = iota((1, zcols), 1)
        place = j // COLUMNS
        away = jnp.where(place % 2 == 1, (place + 1) // 2, -(place // 2))
        aside = (xx + 1) // 2 * (1 - 2 * lax.rem(xx + 1, 2))
        owner = seq_of(lax.rem(z + away + NZ, NZ), x_of(aside), b)
        request = owner * R + lax.rem(j, R)
        pick = (iota((requests, zcols), 0) == request).astype(F32).astype(BF16)
        found = dot(slot, pick)[:1]
        group = (lax.rem(j, COLUMNS) // R).astype(F32)
        key = jnp.where(found > 0.5, group * CAP + found - 1.0, -1.0)
        keys[xx] = jnp.broadcast_to(key, (8, zcols))
        onehot[xx] = (iota((SLOTS, zcols), 0).astype(F32) == key).astype(F32).astype(BF16)

    def private(r):
        keys_here = jnp.concatenate([pk[ptab_ref[r, p]] for p in range(ptab_ref.shape[1])], axis=0)
        values_here = jnp.concatenate([pv[ptab_ref[r, p]] for p in range(ptab_ref.shape[1])], axis=0)
        s = dot_t(q_raw[r], keys_here)
        s = jnp.where(own & (lane // 2 < plen_ref[r]), s, DEAD)
        m = jnp.max(s, axis=1, keepdims=True)
        p = jnp.exp2((s - m) * SCALE)
        l = jnp.sum(p, axis=1, keepdims=True)
        o = dot(p.astype(BF16), values_here) / l
        lse = jnp.where(plen_ref[r] > 0, m * SCALE + jnp.log2(l), DEAD)
        pr_o[pl.ds(r, HEADS, stride=R), :] = o
        pr_l[pl.ds(r, HEADS, stride=R), :] = jnp.broadcast_to(lse, (HEADS, D))

    span = ptab_ref.shape[1] * pk.shape[1]
    lane = iota((HEADS, span), 1)
    own = lax.rem(lane, 2) == iota((HEADS, span), 0) // G

    def all_keys():
        loads["tk"].wait()
        sort_keys(tk_raw, k_te, 0, positions, 0)

    def own_shared():
        sort_keys(sk_raw.at[0], k_sh, 0, half, 0)
        sort_values(sv_raw.at[0], v_sh, 0, half, 0)

    def all_values():
        loads["tv"].wait()
        sort_values(tv_raw, v_te, 0, positions, 0)

    def pair_shared():
        arrived(sk_raw.at[1], pair_s.at[0], pair_r.at[0])
        sort_keys(sk_raw.at[1], k_sh, 0, half, half)
        arrived(sv_raw.at[1], pair_s.at[1], pair_r.at[1])
        sort_values(sv_raw.at[1], v_sh, 0, half, half)

    width = min(256, zcols)

    def shared(i):
        slot, c = i // (zcols // width), lax.rem(i, zcols // width)
        zs = pl.ds(c * (width // COLUMNS), width // COLUMNS)
        into = pl.ds(pl.multiple_of(c * width, width), width)
        scores = [
            dot_t(k_sh[kv], q_all[slot, zs, kv * COLUMNS:(kv + 1) * COLUMNS, :].reshape(width, D))
            for kv in range(KV)
        ]
        for kv, s in enumerate(scores):
            m = jnp.max(s, axis=0, keepdims=True)
            p = jnp.exp2((s - m) * SCALE)
            l = jnp.sum(p, axis=0, keepdims=True)
            sh_o[slot, kv, :, into] = dot(v_sh[kv], p.astype(BF16)) * (1.0 / l)
            sh_l[slot, kv, :, into] = jnp.broadcast_to(m * SCALE + jnp.log2(l), (8, width))

    per_slot = zcols // width

    def loop(first, last, body, unroll=1):
        def step(i, carry):
            body(i)
            return carry

        lax.fori_loop(first, last, step, 0, unroll=unroll)

    for slot_at in range(NX):
        mark(slot_at)
    z_wait(q_all, qz_s, qz_r, 1)
    forward(1)
    all_keys()
    for group in range(2, len(groups)):
        z_wait(q_all, qz_s, qz_r, group)
        forward(group)
    loads["w"].wait()
    go(w.at[0, 0], w.at[0, 1], pair_s.at[2], pair_r.at[2], pair)
    own_shared()
    all_values()
    loads["pk"].wait()
    loads["pv"].wait()
    for r in range(R):
        private(r)
    pair_shared()
    for slot_at in (2, 1, 3):
        x_wait(slot_at)

    def chunk_queries(xx, kv):
        return q_all[xx, :, kv * COLUMNS:(kv + 1) * COLUMNS, :].reshape(zcols, D)

    for kv in range(KV):
        total = dot(onehot[0], chunk_queries(0, kv))
        for xx in range(1, NX):
            total += dot(onehot[xx], chunk_queries(xx, kv))
        qt_send[kv] = total.astype(BF16)

    go(qt_send, qt_recv, pair_s.at[3], pair_r.at[3], pair)

    go(w.at[0, 0], w.at[2, 0], wx_s.at[0], wx_r.at[0], right)
    go(w.at[0, 0], w.at[1, 0], wx_s.at[1], wx_r.at[1], left)
    loop(0, 2 * per_slot, shared)

    extent = tlen_ref[tenant] - lax.rem(seq, 4) * positions
    step_size = min(1024, positions)

    arrived(w.at[0, 1], pair_s.at[2], pair_r.at[2])
    go(w.at[0, 1], w.at[2, 1], wx_s.at[4], wx_r.at[4], right)
    go(w.at[0, 1], w.at[1, 1], wx_s.at[5], wx_r.at[5], left)
    arrived(qt_recv, pair_s.at[3], pair_r.at[3])
    for kv in range(KV):
        qt_recv[kv] = (qt_send[kv].astype(F32) + qt_recv[kv].astype(F32)).astype(BF16)
    te_m[...] = jnp.full(te_m.shape, DEAD, F32)
    te_l[...] = jnp.zeros(te_l.shape, F32)
    te_own[...] = jnp.zeros(te_own.shape, F32)

    def tenant_step(i):
        base = pl.multiple_of(i * step_size, step_size)
        scores = [dot_t(k_te[kv, pl.ds(base, step_size), :], qt_recv[kv]) for kv in range(KV)]
        for kv, s in enumerate(scores):
            s = jnp.where(iota((step_size, SLOTS), 0) < extent - base, s, DEAD)
            m_old = te_m[kv, :1]
            m = jnp.maximum(m_old, jnp.max(s, axis=0, keepdims=True))
            p = jnp.exp2((s - m) * SCALE)
            keep = jnp.exp2((m_old - m) * SCALE)
            te_m[kv, :1] = m
            te_l[kv, :1] = te_l[kv, :1] * keep + jnp.sum(p, axis=0, keepdims=True)
            te_own[kv] = te_own[kv] * keep + dot(v_te[kv, :, pl.ds(base, step_size)], p.astype(BF16))

    loop(0, positions // step_size, tenant_step)
    for kv in range(KV):
        l = te_l[kv, :1]
        o = te_own[kv] * (1.0 / l)
        lse = jnp.where(extent > 0, te_m[kv, :1] * SCALE + jnp.log2(l), DEAD)
        te_own[kv] = o
        te_l[kv, :1] = lse
        to_send[kv, :D] = o.astype(BF16)
        to_send[kv, D:] = split3(lse)
    go(to_send, to_recv, pair_s.at[4], pair_r.at[4], pair)
    loop(2 * per_slot, 4 * per_slot, shared)

    arrived(to_recv, pair_s.at[4], pair_r.at[4])
    for kv in range(KV):
        o, lse = combine([
            (te_l[kv, :1], lambda: te_own[kv]),
            (join3(to_recv[kv, D:]), lambda: to_recv[kv, :D]),
        ])
        hi = o.astype(BF16)
        te_all[kv, :D] = hi
        te_all[kv, D:2 * D] = (o - hi.astype(F32)).astype(BF16)
        te_all[kv, 2 * D:] = split3(lse)

    near = zcols // 2

    def merge(slot, side, extra=False):
        cut = pl.ds(pl.multiple_of(side * near, near), near)
        spread = onehot[slot, :, cut]
        here = keys[slot, :1, cut] >= 0.0
        height = 2 * D + STAT
        parts = dot(te_all[...].reshape(KV * height, SLOTS), spread)
        for kv in range(KV):
            own_part = parts[kv * height:(kv + 1) * height]
            lse = jnp.where(here, join3(own_part[2 * D:]), DEAD)
            pieces = [
                (sh_l[slot, kv, :1, cut], lambda: sh_o[slot, kv, :, cut]),
                (lse, lambda: own_part[:D] + own_part[D:2 * D]),
            ]
            if extra:
                pieces.append((join3(xo_half[side, kv, D:, :]), lambda: xo_half[side, kv, :D, :]))
            o, lse = combine(pieces)
            if isinstance(slot, int) and slot == 0:
                sh_o[0, kv, :, cut] = o
                sh_l[0, kv, :, cut] = jnp.broadcast_to(lse, (8, near))
            else:
                xo_send[slot - 1, kv, :D, cut] = o.astype(BF16)
                xo_send[slot - 1, kv, D:, cut] = split3(lse)

    for side, to in ((0, right), (1, left)):
        merge(3, side)
        half_cut = pl.ds(side * near, near)
        go(xo_send.at[2, :, :, half_cut], xo_half.at[side], xo_s.at[side], xo_r.at[side], to)
    loop(0, 2, lambda i: merge(1 + i, 1 - i))
    loop(0, 2, lambda i: merge(0, i))
    for side, to in ((0, right), (1, left)):
        arrived(xo_half.at[side], xo_s.at[side], xo_r.at[side])
        merge(1 + side, side, True)
        go(xo_send.at[side], xo_full.at[side], xo_s.at[2 + side], xo_r.at[2 + side], to)
    private_o = pr_o[...].T
    private_l = pr_l[...].T[:1]
    for side in range(2):
        arrived(xo_full.at[side], xo_s.at[2 + side], xo_r.at[2 + side])

    both = 2 * COLUMNS
    low = iota((D, both), 1) < COLUMNS

    def join(i):
        cut = pl.ds(pl.multiple_of(i * both, both), both)
        halves, marks = [], []
        for kv in range(KV):
            pieces = [(sh_l[0, kv, :1, cut], lambda: sh_o[0, kv, :, cut])]
            for side in range(2):
                pieces.append((
                    join3(xo_full[side, kv, D:, cut]),
                    lambda side=side: xo_full[side, kv, :D, cut],
                ))
            o, lse = combine(pieces)
            halves.append(o)
            marks.append(jnp.broadcast_to(lse, (8, both)))
        first_o = jnp.where(low, halves[0], pltpu.roll(halves[1], COLUMNS, 1))
        first_l = jnp.where(low[:8], marks[0], pltpu.roll(marks[1], COLUMNS, 1))
        second_o = jnp.where(low, pltpu.roll(halves[0], COLUMNS, 1), halves[1])
        second_l = jnp.where(low[:8], pltpu.roll(marks[0], COLUMNS, 1), marks[1])
        for p, o, lse in ((2 * i, first_o, first_l), (2 * i + 1, second_o, second_l)):
            zo_send[p, :D] = o.astype(BF16)
            zo_send[p, D:] = split3(lse[:1])

        @pl.when(i == 0)
        def _():
            zo_own[...] = first_o
            zl_own[...] = first_l

    loop(0, zcols // both, join, zcols // both)
    for p in range(1, NZ):
        q = back(p)
        to = device(z_of(zorder[p]), x, b, h)
        go(zo_send.at[p], zo_recv.at[q - 1], zo_s.at[p - 1], zo_r.at[q - 1], to)

    arrived(w.at[2, 0], wx_s.at[0], wx_r.at[0])
    go(w.at[2, 0], w.at[3, 0], wx_s.at[2], wx_r.at[2], right)
    arrived(w.at[1, 1], wx_s.at[5], wx_r.at[5])
    go(w.at[1, 1], w.at[3, 1], wx_s.at[3], wx_r.at[3], left)

    pieces = [(private_l, lambda: private_o), (zl_own[:1], lambda: zo_own[...])]
    for p in range(1, NZ):
        arrived(zo_recv.at[p - 1], zo_s.at[p - 1], zo_r.at[p - 1])
        pieces.append((join3(zo_recv[p - 1, D:]), lambda p=p: zo_recv[p - 1, :D]))
    attended, _ = combine(pieces)
    at[0, 0] = attended.T.astype(BF16)

    z_start(at, az_s, az_r)
    for group in range(len(groups)):
        z_wait(at, az_s, az_r, group)
    wide = at[0].astype(F32)
    rows = jnp.concatenate([
        wide[:, i * R:(i + 1) * R, :].reshape(NZ * R, D).astype(BF16) for i in range(HEADS)
    ], axis=1)
    arrived(w.at[2, 1], wx_s.at[4], wx_r.at[4])
    arrived(w.at[1, 0], wx_s.at[1], wx_r.at[1])
    arrived(w.at[3, 0], wx_s.at[2], wx_r.at[2])
    arrived(w.at[3, 1], wx_s.at[3], wx_r.at[3])
    def project(slot):
        sums = dot(rows, jnp.concatenate([w[slot, 0], w[slot, 1]], axis=1))
        for db in range(2):
            for p in range(NZ):
                part[db, z_of(zorder[p]), slot] = sums[p * R:(p + 1) * R, db * D:(db + 1) * D]

    loop(0, NX, project, NX)

    for k in range(1, 2 * NH):
        dh, db = k // 2, k % 2
        src = part.at[db, pl.ds(h_of(dh) * zper, zper)]
        go(src, rs_recv.at[k - 1], rs_s.at[k - 1], rs_r.at[k - 1], device(z, x, b_of(db), h_of(dh)))
    totals = [part[0, pl.ds(h * zper, zper)], None]
    for k in range(1, 2 * NH):
        arrived(rs_recv.at[k - 1], rs_s.at[k - 1], rs_r.at[k - 1])
        got = rs_recv[k - 1]
        totals[k % 2] = got if totals[k % 2] is None else totals[k % 2] + got
    first = jnp.where(b == 0, totals[0], totals[1])
    second = jnp.where(b == 0, totals[1], totals[0])

    for slot, to in ((3, far), (1, right), (2, left), (0, None)):
        rows = jnp.concatenate([first[:, slot], second[:, slot]], axis=1).astype(BF16)
        if to is None:
            final[:, x] = rows
        else:
            fx_send[slot - 1] = rows
            k = slot - 1
            go(fx_send.at[k], final.at[:, x], fx_s.at[k], fx_r.at[k], to)
    for slot, offset in ((3, 2), (1, -1), (2, 1)):
        arrived(final.at[:, x_of(offset)], fx_s.at[slot - 1], fx_r.at[slot - 1])
    out_ref[...] = final[...].reshape(zper * NX * 2 * R, D)

    for copy in started:
        copy.wait_send()


def local(NZ, NX, NH, queries, sk, sv, tk, tv, ids, tlen, plen, ptab, pk, pv, w):
    flat = lambda rows: rows.reshape(rows.shape[0] * KV, D)
    paged = lambda rows: rows.reshape(rows.shape[0], rows.shape[1] * KV, D)
    sk, sv, tk, tv = flat(sk), flat(sv), flat(tk), flat(tv)
    pk, pv = paged(pk), paged(pv)
    shared2, positions = sk.shape[0], tk.shape[0] // KV
    zcols = NZ * COLUMNS
    zper = NZ // NH
    dma = pltpu.SemaphoreType.DMA
    v = pltpu.VMEM
    scratch = [
        v(queries.shape, BF16), v((R * HEADS, D), F32),
        v((2, shared2, D), BF16), v((2, shared2, D), BF16), v(tk.shape, BF16), v(tv.shape, BF16),
        v(pk.shape, BF16), v(pv.shape, BF16), v((NX, 2) + w.shape, BF16),
        v((KV, shared2, D), BF16), v((KV, D, shared2), BF16),
        v((KV, positions, D), BF16), v((KV, D, positions), BF16),
        v((NX, NZ, R * HEADS, D), BF16), v((NX, SLOTS, zcols), BF16), v((NX, 8, zcols), F32),
        v((KV, SLOTS, D), BF16), v((KV, SLOTS, D), BF16),
        v((KV, 8, SLOTS), F32), v((KV, 8, SLOTS), F32), v((KV, D, SLOTS), F32),
        v((KV, D + STAT, SLOTS), BF16), v((KV, D + STAT, SLOTS), BF16),
        v((KV, 2 * D + STAT, SLOTS), BF16),
        v((NX, KV, D, zcols), F32), v((NX, KV, 8, zcols), F32),
        v((3, KV, D + STAT, zcols), BF16), v((2, KV, D + STAT, zcols // 2), BF16),
        v((2, KV, D + STAT, zcols), BF16),
        v((D, R * HEADS), F32), v((8, R * HEADS), F32),
        v((NZ, D + STAT, R * HEADS), BF16), v((NZ - 1, D + STAT, R * HEADS), BF16),
        v((R * HEADS, D), F32), v((R * HEADS, D), F32),
        v((1, NZ, R * HEADS, D), BF16), v((2, NZ, NX, R, D), F32),
        v((2 * NH - 1, zper, NX, R, D), F32),
        v((NX - 1, zper, 2 * R, D), BF16), v((zper, NX, 2 * R, D), BF16),
        dma((8,)),
    ]
    for count in (NZ - 1, 9, 5, 4, NZ - 1, NZ - 1, 6, 2 * NH - 1, NX - 1):
        scratch += [dma((count,)), dma((count,))]
    hbm = pl.BlockSpec(memory_space=pl.ANY)
    smem = pl.BlockSpec(memory_space=pltpu.SMEM)
    vmem = pl.BlockSpec(memory_space=pltpu.VMEM)
    return pl.pallas_call(
        functools.partial(kernel, NZ, NX, NH),
        out_shape=jax.ShapeDtypeStruct((zper * NX * 2 * R, D), BF16),
        in_specs=[hbm] * 5 + [vmem, smem, smem, smem] + [hbm] * 3,
        out_specs=vmem,
        scratch_shapes=scratch,
        compiler_params=pltpu.CompilerParams(
            collective_id=0, has_side_effects=True, vmem_limit_bytes=56 * 1024 * 1024
        ),
    )(queries, sk, sv, tk, tv, ids.reshape(1, -1), tlen, plen, ptab, pk, pv, w)


def solution(mesh):
    sizes = dict(mesh.shape)
    NX = 4
    NZ = sizes["seq"] // (2 * NX)
    placed = (
        P("seq", "head", None),
        P("seq", "head", None),
        P("seq", "head", None),
        P("seq", "head", None),
        P("seq", "head", None),
        P(),
        P(),
        P("seq"),
        P("seq", None),
        P("seq", None, "head", None),
        P("seq", None, "head", None),
        P("head", "seq"),
    )
    return jax.shard_map(
        functools.partial(local, NZ, NX, sizes["head"]),
        mesh=mesh, in_specs=placed, out_specs=P("head", "seq"), check_vma=False,
    )
```

```python
import functools
import math

import jax
import jax.numpy as jnp
from jax import lax
from jax.experimental import pallas as pl
from jax.experimental.pallas import tpu as pltpu
from jax.sharding import PartitionSpec as P

MESH = pl.DeviceIdType.MESH
F32 = jnp.float32
BF16 = jnp.bfloat16
DEAD = -1e30
KV = 2
G = 8
D = 128
R = 8
HEADS = KV * G
STAT = 16
CAP = 48
SLOTS = CAP * G
COLUMNS = R * G
LOG2E = math.log2(math.e)
SCALE = LOG2E / math.sqrt(D)


def dot(a, b):
    return jnp.dot(a, b, preferred_element_type=F32)


def dot_t(a, b):
    return lax.dot_general(a, b, (((1,), (1,)), ((), ())), preferred_element_type=F32)


def split3(v):
    terms = []
    for _ in range(3):
        term = v.astype(BF16).astype(F32)
        terms.append(term)
        v = v - term
    terms.append(jnp.zeros((STAT - 3, v.shape[1]), F32))
    return jnp.concatenate(terms, axis=0).astype(BF16)


def join3(rows):
    rows = rows.astype(F32)
    return rows[0:1] + rows[1:2] + rows[2:3]


def combine(pieces):
    top = pieces[0][0]
    for lse, _ in pieces[1:]:
        top = jnp.maximum(top, lse)
    weights = [jnp.exp2(lse - top) for lse, _ in pieces]
    whole = functools.reduce(lambda one, two: one + two, weights)
    inverse = 1.0 / whole
    total = None
    for weight, (_, o) in zip(weights, pieces):
        term = o().astype(F32) * (weight * inverse)
        total = term if total is None else total + term
    return total, top + jnp.log2(whole)


def iota(shape, axis):
    return lax.broadcasted_iota(jnp.int32, shape, axis)


def kernel(
    NZ, NX, NH,
    q_hbm, sk_hbm, sv_hbm, tk_hbm, tv_hbm, ids_ref, tlen_ref, plen_ref, ptab_ref,
    pk_hbm, pv_hbm, w_hbm, out_ref,
    q_raw, q_wide, sk_raw, sv_raw, tk_raw, tv_raw, pk, pv, w,
    k_sh, v_sh, k_te, v_te,
    q_all, onehot, keys, qt_send, qt_recv,
    te_m, te_l, te_own, to_send, to_recv,
    te_all, sh_o, sh_l,
    xo_send, xo_half, xo_full, zo_own, zl_own, zo_send, zo_recv,
    pr_o, pr_l, at, part, rs_recv, fx_send, final,
    in_sem,
    qz_s, qz_r, qx_s, qx_r, pair_s, pair_r, xo_s, xo_r,
    zo_s, zo_r, az_s, az_r, wx_s, wx_r, rs_s, rs_r, fx_s, fx_r,
):
    seq = lax.axis_index("seq")
    h = lax.axis_index("head")
    b = lax.rem(seq, 2)
    x = lax.rem(seq // 2, NX)
    z = seq // (2 * NX)
    pages = pk.shape[0]
    zcols = NZ * COLUMNS
    zper = NZ // NH

    def seq_of(zz, xx, bb):
        return (zz * NX + xx) * 2 + bb

    def device(zz, xx, bb, hh):
        return {"seq": seq_of(zz, xx, bb), "head": hh}

    zorder = [(p + 1) // 2 if p % 2 else -(p // 2) for p in range(NZ)]
    xorder = [0, 1, -1, 2]
    cuts = [0, 1, 5, 8] if NZ == 8 else [0, 1, NZ]
    groups = list(zip(cuts[:-1], cuts[1:]))

    def back(p):
        return [(zorder[p] + other) % NZ for other in zorder].index(0)

    def z_of(dz):
        return lax.rem(z + dz + NZ, NZ)

    def x_of(dx):
        return lax.rem(x + dx + NX, NX)

    def h_of(dh):
        return lax.rem(h + dh + NH, NH)

    def b_of(db):
        return lax.rem(b + db, 2)

    def send(src, dst, s, r, dev):
        return pltpu.make_async_remote_copy(
            src_ref=src, dst_ref=dst, send_sem=s, recv_sem=r, device_id=dev, device_id_type=MESH
        )

    me = device(z, x, b, h)
    pair = device(z, x, b_of(1), h)
    started = []

    def go(*args):
        copy = send(*args)
        copy.start()
        started.append(copy)

    def arrived(ref, s, r):
        send(ref, ref, s, r, pair).wait_recv()

    loads = {}
    for at_sem, (name, src, dst) in enumerate((
        ("q", q_hbm, q_raw),
        ("sk", sk_hbm, sk_raw.at[0]),
        ("sv", sv_hbm, sv_raw.at[0]),
        ("tk", tk_hbm, tk_raw),
        ("tv", tv_hbm, tv_raw),
        ("pk", pk_hbm, pk),
        ("pv", pv_hbm, pv),
        ("w", w_hbm, w.at[0, 0]),
    )):
        loads[name] = pltpu.make_async_copy(src, dst, in_sem.at[at_sem])
        loads[name].start()

    barrier = pltpu.get_barrier_semaphore()
    peers = [device(z_of(dz), x, b, h) for dz in range(1, NZ)]
    peers += [device(z, x_of(dx), b, h) for dx in range(1, NX)]
    peers += [
        device(z, x, b_of(db), h_of(dh)) for dh in range(NH) for db in range(2) if dh + db > 0
    ]
    for peer in peers:
        pl.semaphore_signal(barrier, inc=1, device_id=peer, device_id_type=MESH)

    loads["q"].wait()
    q_wide[...] = q_raw[...].astype(F32).reshape(R * HEADS, D)
    q_all[0, 0] = jnp.concatenate(
        [q_wide[pl.ds(i, R, stride=HEADS), :] for i in range(HEADS)], axis=0
    ).astype(BF16)

    pl.semaphore_wait(barrier, len(peers))

    left, right, far = device(z, x_of(-1), b, h), device(z, x_of(1), b, h), device(z, x_of(2), b, h)

    def z_start(buf, zs, zr):
        for p in range(1, NZ):
            q = back(p)
            go(buf.at[0, 0], buf.at[0, q], zs.at[p - 1], zr.at[q - 1], device(z_of(zorder[p]), x, b, h))

    def z_wait(buf, zs, zr, group):
        for p in range(*groups[group]):
            if p > 0:
                arrived(buf.at[0, p], zs.at[p - 1], zr.at[p - 1])

    def block(slot, group):
        first, last = groups[group]
        return q_all.at[slot, pl.ds(first, last - first)]

    def forward(group):
        for slot, to in ((2, right), (1, left), (3, far)):
            k = 3 * group + slot - 1
            go(block(0, group), block(slot, group), qx_s.at[k], qx_r.at[k], to)

    def x_wait(slot):
        for group in range(len(groups)):
            k = 3 * group + slot - 1
            arrived(block(slot, group), qx_s.at[k], qx_r.at[k])

    z_start(q_all, qz_s, qz_r)
    forward(0)
    loads["sk"].wait()
    go(sk_raw.at[0], sk_raw.at[1], pair_s.at[0], pair_r.at[0], pair)
    loads["sv"].wait()
    go(sv_raw.at[0], sv_raw.at[1], pair_s.at[1], pair_r.at[1], pair)

    row, col = iota((2 * D, 2 * D), 0), iota((2 * D, 2 * D), 1)
    sort = (col == jnp.where(row < D, 2 * row, 2 * (row - D) + 1)).astype(F32).astype(BF16)

    def sort_keys(raw, into, first, last, base):
        def step(i, carry):
            at_row = pl.multiple_of(i * 2 * D, 2 * D)
            to_row = pl.multiple_of(base + i * D, D)
            rows = dot(sort, raw[pl.ds(at_row, 2 * D), :]).astype(BF16)
            into[0, pl.ds(to_row, D), :] = rows[:D]
            into[1, pl.ds(to_row, D), :] = rows[D:]
            return carry

        lax.fori_loop(first // D, last // D, step, 0, unroll=4)

    def sort_values(raw, into, first, last, base):
        def step(i, carry):
            at_row = pl.multiple_of(i * 2 * D, 2 * D)
            to_row = pl.multiple_of(base + i * D, D)
            rows = dot(sort, raw[pl.ds(at_row, 2 * D), :])
            into[0, :, pl.ds(to_row, D)] = rows[:D].T.astype(BF16)
            into[1, :, pl.ds(to_row, D)] = rows[D:].T.astype(BF16)
            return carry

        lax.fori_loop(first // D, last // D, step, 0, unroll=4)

    positions = k_te.shape[1]
    half = sk_raw.shape[1] // 2

    tenant = seq // 4
    requests = ids_ref.shape[1]
    match = (ids_ref[...] == tenant).astype(F32)
    match = jnp.broadcast_to(match, (16, requests))
    upto = (iota((requests, requests), 0) <= iota((requests, requests), 1)).astype(F32).astype(BF16)
    slot = (match * dot(match.astype(BF16), upto)).astype(BF16)

    def mark(xx):
        j = iota((1, zcols), 1)
        place = j // COLUMNS
        away = jnp.where(place % 2 == 1, (place + 1) // 2, -(place // 2))
        aside = (xx + 1) // 2 * (1 - 2 * lax.rem(xx + 1, 2))
        owner = seq_of(lax.rem(z + away + NZ, NZ), x_of(aside), b)
        request = owner * R + lax.rem(j, R)
        pick = (iota((requests, zcols), 0) == request).astype(F32).astype(BF16)
        found = dot(slot, pick)[:1]
        group = (lax.rem(j, COLUMNS) // R).astype(F32)
        key = jnp.where(found > 0.5, group * CAP + found - 1.0, -1.0)
        keys[xx] = jnp.broadcast_to(key, (8, zcols))
        onehot[xx] = (iota((SLOTS, zcols), 0).astype(F32) == key).astype(F32).astype(BF16)

    def private(r):
        keys_here = jnp.concatenate([pk[ptab_ref[r, p]] for p in range(ptab_ref.shape[1])], axis=0)
        values_here = jnp.concatenate([pv[ptab_ref[r, p]] for p in range(ptab_ref.shape[1])], axis=0)
        s = dot_t(q_raw[r], keys_here)
        s = jnp.where(own & (lane // 2 < plen_ref[r]), s, DEAD)
        m = jnp.max(s, axis=1, keepdims=True)
        p = jnp.exp2((s - m) * SCALE)
        l = jnp.sum(p, axis=1, keepdims=True)
        o = dot(p.astype(BF16), values_here) / l
        lse = jnp.where(plen_ref[r] > 0, m * SCALE + jnp.log2(l), DEAD)
        pr_o[pl.ds(r, HEADS, stride=R), :] = o
        pr_l[pl.ds(r, HEADS, stride=R), :] = jnp.broadcast_to(lse, (HEADS, D))

    span = ptab_ref.shape[1] * pk.shape[1]
    lane = iota((HEADS, span), 1)
    own = lax.rem(lane, 2) == iota((HEADS, span), 0) // G

    def all_keys():
        loads["tk"].wait()
        sort_keys(tk_raw, k_te, 0, positions, 0)

    def own_shared():
        sort_keys(sk_raw.at[0], k_sh, 0, half, 0)
        sort_values(sv_raw.at[0], v_sh, 0, half, 0)

    def all_values():
        loads["tv"].wait()
        sort_values(tv_raw, v_te, 0, positions, 0)

    def pair_shared():
        arrived(sk_raw.at[1], pair_s.at[0], pair_r.at[0])
        sort_keys(sk_raw.at[1], k_sh, 0, half, half)
        arrived(sv_raw.at[1], pair_s.at[1], pair_r.at[1])
        sort_values(sv_raw.at[1], v_sh, 0, half, half)

    width = min(256, zcols)

    def shared(i):
        slot, c = i // (zcols // width), lax.rem(i, zcols // width)
        zs = pl.ds(c * (width // COLUMNS), width // COLUMNS)
        into = pl.ds(pl.multiple_of(c * width, width), width)
        scores = [
            dot_t(k_sh[kv], q_all[slot, zs, kv * COLUMNS:(kv + 1) * COLUMNS, :].reshape(width, D))
            for kv in range(KV)
        ]
        for kv, s in enumerate(scores):
            m = jnp.max(s, axis=0, keepdims=True)
            p = jnp.exp2((s - m) * SCALE)
            l = jnp.sum(p, axis=0, keepdims=True)
            sh_o[slot, kv, :, into] = dot(v_sh[kv], p.astype(BF16)) * (1.0 / l)
            sh_l[slot, kv, :, into] = jnp.broadcast_to(m * SCALE + jnp.log2(l), (8, width))

    per_slot = zcols // width

    def loop(first, last, body, unroll=1):
        def step(i, carry):
            body(i)
            return carry

        lax.fori_loop(first, last, step, 0, unroll=unroll)

    for slot_at in range(NX):
        mark(slot_at)
    z_wait(q_all, qz_s, qz_r, 1)
    forward(1)
    all_keys()
    for group in range(2, len(groups)):
        z_wait(q_all, qz_s, qz_r, group)
        forward(group)
    loads["w"].wait()
    go(w.at[0, 0], w.at[0, 1], pair_s.at[2], pair_r.at[2], pair)
    own_shared()
    all_values()
    loads["pk"].wait()
    loads["pv"].wait()
    for r in range(R):
        private(r)
    pair_shared()
    for slot_at in (2, 1, 3):
        x_wait(slot_at)

    def chunk_queries(xx, kv):
        return q_all[xx, :, kv * COLUMNS:(kv + 1) * COLUMNS, :].reshape(zcols, D)

    for kv in range(KV):
        total = dot(onehot[0], chunk_queries(0, kv))
        for xx in range(1, NX):
            total += dot(onehot[xx], chunk_queries(xx, kv))
        qt_send[kv] = total.astype(BF16)

    go(qt_send, qt_recv, pair_s.at[3], pair_r.at[3], pair)

    go(w.at[0, 0], w.at[2, 0], wx_s.at[0], wx_r.at[0], right)
    go(w.at[0, 0], w.at[1, 0], wx_s.at[1], wx_r.at[1], left)
    loop(0, 2 * per_slot, shared)

    extent = tlen_ref[tenant] - lax.rem(seq, 4) * positions
    step_size = min(1024, positions)

    arrived(w.at[0, 1], pair_s.at[2], pair_r.at[2])
    go(w.at[0, 1], w.at[2, 1], wx_s.at[4], wx_r.at[4], right)
    go(w.at[0, 1], w.at[1, 1], wx_s.at[5], wx_r.at[5], left)
    arrived(qt_recv, pair_s.at[3], pair_r.at[3])
    for kv in range(KV):
        qt_recv[kv] = (qt_send[kv].astype(F32) + qt_recv[kv].astype(F32)).astype(BF16)
    te_m[...] = jnp.full(te_m.shape, DEAD, F32)
    te_l[...] = jnp.zeros(te_l.shape, F32)
    te_own[...] = jnp.zeros(te_own.shape, F32)

    def tenant_step(i):
        base = pl.multiple_of(i * step_size, step_size)
        scores = [dot_t(k_te[kv, pl.ds(base, step_size), :], qt_recv[kv]) for kv in range(KV)]
        for kv, s in enumerate(scores):
            s = jnp.where(iota((step_size, SLOTS), 0) < extent - base, s, DEAD)
            m_old = te_m[kv, :1]
            m = jnp.maximum(m_old, jnp.max(s, axis=0, keepdims=True))
            p = jnp.exp2((s - m) * SCALE)
            keep = jnp.exp2((m_old - m) * SCALE)
            te_m[kv, :1] = m
            te_l[kv, :1] = te_l[kv, :1] * keep + jnp.sum(p, axis=0, keepdims=True)
            te_own[kv] = te_own[kv] * keep + dot(v_te[kv, :, pl.ds(base, step_size)], p.astype(BF16))

    loop(0, positions // step_size, tenant_step)
    for kv in range(KV):
        l = te_l[kv, :1]
        o = te_own[kv] * (1.0 / l)
        lse = jnp.where(extent > 0, te_m[kv, :1] * SCALE + jnp.log2(l), DEAD)
        te_own[kv] = o
        te_l[kv, :1] = lse
        to_send[kv, :D] = o.astype(BF16)
        to_send[kv, D:] = split3(lse)
    go(to_send, to_recv, pair_s.at[4], pair_r.at[4], pair)
    loop(2 * per_slot, 4 * per_slot, shared)

    arrived(to_recv, pair_s.at[4], pair_r.at[4])
    for kv in range(KV):
        o, lse = combine([
            (te_l[kv, :1], lambda: te_own[kv]),
            (join3(to_recv[kv, D:]), lambda: to_recv[kv, :D]),
        ])
        hi = o.astype(BF16)
        te_all[kv, :D] = hi
        te_all[kv, D:2 * D] = (o - hi.astype(F32)).astype(BF16)
        te_all[kv, 2 * D:] = split3(lse)

    near = zcols // 2

    def merge(slot, side, extra=False):
        cut = pl.ds(pl.multiple_of(side * near, near), near)
        spread = onehot[slot, :, cut]
        here = keys[slot, :1, cut] >= 0.0
        height = 2 * D + STAT
        parts = dot(te_all[...].reshape(KV * height, SLOTS), spread)
        for kv in range(KV):
            own_part = parts[kv * height:(kv + 1) * height]
            lse = jnp.where(here, join3(own_part[2 * D:]), DEAD)
            pieces = [
                (sh_l[slot, kv, :1, cut], lambda: sh_o[slot, kv, :, cut]),
                (lse, lambda: own_part[:D] + own_part[D:2 * D]),
            ]
            if extra:
                pieces.append((join3(xo_half[side, kv, D:, :]), lambda: xo_half[side, kv, :D, :]))
            o, lse = combine(pieces)
            if isinstance(slot, int) and slot == 0:
                sh_o[0, kv, :, cut] = o
                sh_l[0, kv, :, cut] = jnp.broadcast_to(lse, (8, near))
            else:
                xo_send[slot - 1, kv, :D, cut] = o.astype(BF16)
                xo_send[slot - 1, kv, D:, cut] = split3(lse)

    for side, to in ((0, right), (1, left)):
        merge(3, side)
        half_cut = pl.ds(side * near, near)
        go(xo_send.at[2, :, :, half_cut], xo_half.at[side], xo_s.at[side], xo_r.at[side], to)
    for side, to in ((0, right), (1, left)):
        merge(1 + side, 1 - side)
        half_cut = pl.ds((1 - side) * near, near)
        go(xo_send.at[side, :, :, half_cut], xo_full.at[side, :, :, half_cut], xo_s.at[2 + side], xo_r.at[2 + side], to)
    loop(0, 2, lambda i: merge(0, i))
    for side, to in ((0, right), (1, left)):
        arrived(xo_half.at[side], xo_s.at[side], xo_r.at[side])
        merge(1 + side, side, True)
        half_cut = pl.ds(side * near, near)
        go(xo_send.at[side, :, :, half_cut], xo_full.at[side, :, :, half_cut], xo_s.at[4 + side], xo_r.at[4 + side], to)
    private_o = pr_o[...].T
    private_l = pr_l[...].T[:1]
    for k, side, part_at in ((2, 0, 1), (3, 1, 0), (4, 0, 0), (5, 1, 1)):
        arrived(xo_full.at[side, :, :, pl.ds(part_at * near, near)], xo_s.at[k], xo_r.at[k])

    both = 2 * COLUMNS
    low = iota((D, both), 1) < COLUMNS

    def join(i):
        cut = pl.ds(i * both, both)
        halves, marks = [], []
        for kv in range(KV):
            pieces = [(sh_l[0, kv, :1, cut], lambda: sh_o[0, kv, :, cut])]
            for side in range(2):
                pieces.append((
                    join3(xo_full[side, kv, D:, cut]),
                    lambda side=side: xo_full[side, kv, :D, cut],
                ))
            o, lse = combine(pieces)
            halves.append(o)
            marks.append(jnp.broadcast_to(lse, (8, both)))
        first_o = jnp.where(low, halves[0], pltpu.roll(halves[1], COLUMNS, 1))
        first_l = jnp.where(low[:8], marks[0], pltpu.roll(marks[1], COLUMNS, 1))
        second_o = jnp.where(low, pltpu.roll(halves[0], COLUMNS, 1), halves[1])
        second_l = jnp.where(low[:8], pltpu.roll(marks[0], COLUMNS, 1), marks[1])
        for p, o, lse in ((2 * i, first_o, first_l), (2 * i + 1, second_o, second_l)):
            zo_send[p, :D] = o.astype(BF16)
            zo_send[p, D:] = split3(lse[:1])
            if p == 0:
                zo_own[...] = o
                zl_own[...] = lse
            else:
                q = back(p)
                to = device(z_of(zorder[p]), x, b, h)
                go(zo_send.at[p], zo_recv.at[q - 1], zo_s.at[p - 1], zo_r.at[q - 1], to)

    for i in reversed(range(zcols // both)):
        join(i)

    arrived(w.at[2, 0], wx_s.at[0], wx_r.at[0])
    go(w.at[2, 0], w.at[3, 0], wx_s.at[2], wx_r.at[2], right)
    arrived(w.at[1, 1], wx_s.at[5], wx_r.at[5])
    go(w.at[1, 1], w.at[3, 1], wx_s.at[3], wx_r.at[3], left)

    pieces = [(private_l, lambda: private_o), (zl_own[:1], lambda: zo_own[...])]
    for p in range(1, NZ):
        arrived(zo_recv.at[p - 1], zo_s.at[p - 1], zo_r.at[p - 1])
        pieces.append((join3(zo_recv[p - 1, D:]), lambda p=p: zo_recv[p - 1, :D]))
    attended, _ = combine(pieces)
    at[0, 0] = attended.T.astype(BF16)

    z_start(at, az_s, az_r)
    for group in range(len(groups)):
        z_wait(at, az_s, az_r, group)
    wide = at[0].astype(F32)
    rows = jnp.concatenate([
        wide[:, i * R:(i + 1) * R, :].reshape(NZ * R, D).astype(BF16) for i in range(HEADS)
    ], axis=1)
    arrived(w.at[2, 1], wx_s.at[4], wx_r.at[4])
    arrived(w.at[1, 0], wx_s.at[1], wx_r.at[1])
    arrived(w.at[3, 0], wx_s.at[2], wx_r.at[2])
    arrived(w.at[3, 1], wx_s.at[3], wx_r.at[3])
    def project(slot):
        sums = dot(rows, jnp.concatenate([w[slot, 0], w[slot, 1]], axis=1))
        for db in range(2):
            for p in range(NZ):
                part[db, z_of(zorder[p]), slot] = sums[p * R:(p + 1) * R, db * D:(db + 1) * D]

    loop(0, NX, project, NX)

    for k in range(1, 2 * NH):
        dh, db = k // 2, k % 2
        src = part.at[db, pl.ds(h_of(dh) * zper, zper)]
        go(src, rs_recv.at[k - 1], rs_s.at[k - 1], rs_r.at[k - 1], device(z, x, b_of(db), h_of(dh)))
    totals = [part[0, pl.ds(h * zper, zper)], None]
    for k in range(1, 2 * NH):
        arrived(rs_recv.at[k - 1], rs_s.at[k - 1], rs_r.at[k - 1])
        got = rs_recv[k - 1]
        totals[k % 2] = got if totals[k % 2] is None else totals[k % 2] + got
    first = jnp.where(b == 0, totals[0], totals[1])
    second = jnp.where(b == 0, totals[1], totals[0])

    for slot, to in ((3, far), (1, right), (2, left), (0, None)):
        rows = jnp.concatenate([first[:, slot], second[:, slot]], axis=1).astype(BF16)
        if to is None:
            final[:, x] = rows
        else:
            fx_send[slot - 1] = rows
            k = slot - 1
            go(fx_send.at[k], final.at[:, x], fx_s.at[k], fx_r.at[k], to)
    for slot, offset in ((3, 2), (1, -1), (2, 1)):
        arrived(final.at[:, x_of(offset)], fx_s.at[slot - 1], fx_r.at[slot - 1])
    out_ref[...] = final[...].reshape(zper * NX * 2 * R, D)

    for copy in started:
        copy.wait_send()


def local(NZ, NX, NH, queries, sk, sv, tk, tv, ids, tlen, plen, ptab, pk, pv, w):
    flat = lambda rows: rows.reshape(rows.shape[0] * KV, D)
    paged = lambda rows: rows.reshape(rows.shape[0], rows.shape[1] * KV, D)
    sk, sv, tk, tv = flat(sk), flat(sv), flat(tk), flat(tv)
    pk, pv = paged(pk), paged(pv)
    shared2, positions = sk.shape[0], tk.shape[0] // KV
    zcols = NZ * COLUMNS
    zper = NZ // NH
    dma = pltpu.SemaphoreType.DMA
    v = pltpu.VMEM
    scratch = [
        v(queries.shape, BF16), v((R * HEADS, D), F32),
        v((2, shared2, D), BF16), v((2, shared2, D), BF16), v(tk.shape, BF16), v(tv.shape, BF16),
        v(pk.shape, BF16), v(pv.shape, BF16), v((NX, 2) + w.shape, BF16),
        v((KV, shared2, D), BF16), v((KV, D, shared2), BF16),
        v((KV, positions, D), BF16), v((KV, D, positions), BF16),
        v((NX, NZ, R * HEADS, D), BF16), v((NX, SLOTS, zcols), BF16), v((NX, 8, zcols), F32),
        v((KV, SLOTS, D), BF16), v((KV, SLOTS, D), BF16),
        v((KV, 8, SLOTS), F32), v((KV, 8, SLOTS), F32), v((KV, D, SLOTS), F32),
        v((KV, D + STAT, SLOTS), BF16), v((KV, D + STAT, SLOTS), BF16),
        v((KV, 2 * D + STAT, SLOTS), BF16),
        v((NX, KV, D, zcols), F32), v((NX, KV, 8, zcols), F32),
        v((3, KV, D + STAT, zcols), BF16), v((2, KV, D + STAT, zcols // 2), BF16),
        v((2, KV, D + STAT, zcols), BF16),
        v((D, R * HEADS), F32), v((8, R * HEADS), F32),
        v((NZ, D + STAT, R * HEADS), BF16), v((NZ - 1, D + STAT, R * HEADS), BF16),
        v((R * HEADS, D), F32), v((R * HEADS, D), F32),
        v((1, NZ, R * HEADS, D), BF16), v((2, NZ, NX, R, D), F32),
        v((2 * NH - 1, zper, NX, R, D), F32),
        v((NX - 1, zper, 2 * R, D), BF16), v((zper, NX, 2 * R, D), BF16),
        dma((8,)),
    ]
    for count in (NZ - 1, 9, 5, 6, NZ - 1, NZ - 1, 6, 2 * NH - 1, NX - 1):
        scratch += [dma((count,)), dma((count,))]
    hbm = pl.BlockSpec(memory_space=pl.ANY)
    smem = pl.BlockSpec(memory_space=pltpu.SMEM)
    vmem = pl.BlockSpec(memory_space=pltpu.VMEM)
    return pl.pallas_call(
        functools.partial(kernel, NZ, NX, NH),
        out_shape=jax.ShapeDtypeStruct((zper * NX * 2 * R, D), BF16),
        in_specs=[hbm] * 5 + [vmem, smem, smem, smem] + [hbm] * 3,
        out_specs=vmem,
        scratch_shapes=scratch,
        compiler_params=pltpu.CompilerParams(
            collective_id=0, has_side_effects=True, vmem_limit_bytes=56 * 1024 * 1024
        ),
    )(queries, sk, sv, tk, tv, ids.reshape(1, -1), tlen, plen, ptab, pk, pv, w)


def solution(mesh):
    sizes = dict(mesh.shape)
    NX = 4
    NZ = sizes["seq"] // (2 * NX)
    placed = (
        P("seq", "head", None),
        P("seq", "head", None),
        P("seq", "head", None),
        P("seq", "head", None),
        P("seq", "head", None),
        P(),
        P(),
        P("seq"),
        P("seq", None),
        P("seq", None, "head", None),
        P("seq", None, "head", None),
        P("head", "seq"),
    )
    return jax.shard_map(
        functools.partial(local, NZ, NX, sizes["head"]),
        mesh=mesh, in_specs=placed, out_specs=P("head", "seq"), check_vma=False,
    )
```

```python
import functools
import math

import jax
import jax.numpy as jnp
from jax import lax
from jax.experimental import pallas as pl
from jax.experimental.pallas import tpu as pltpu
from jax.sharding import PartitionSpec as P

MESH = pl.DeviceIdType.MESH
F32 = jnp.float32
BF16 = jnp.bfloat16
DEAD = -1e30
KV = 2
G = 8
D = 128
R = 8
HEADS = KV * G
STAT = 16
CAP = 48
SLOTS = CAP * G
COLUMNS = R * G
LOG2E = math.log2(math.e)
SCALE = LOG2E / math.sqrt(D)


def dot(a, b):
    return jnp.dot(a, b, preferred_element_type=F32)


def dot_t(a, b):
    return lax.dot_general(a, b, (((1,), (1,)), ((), ())), preferred_element_type=F32)


def split3(v):
    terms = []
    for _ in range(3):
        term = v.astype(BF16).astype(F32)
        terms.append(term)
        v = v - term
    terms.append(jnp.zeros((STAT - 3, v.shape[1]), F32))
    return jnp.concatenate(terms, axis=0).astype(BF16)


def join3(rows):
    rows = rows.astype(F32)
    return rows[0:1] + rows[1:2] + rows[2:3]


def combine(pieces):
    top = pieces[0][0]
    for lse, _ in pieces[1:]:
        top = jnp.maximum(top, lse)
    weights = [jnp.exp2(lse - top) for lse, _ in pieces]
    whole = functools.reduce(lambda one, two: one + two, weights)
    inverse = 1.0 / whole
    total = None
    for weight, (_, o) in zip(weights, pieces):
        term = o().astype(F32) * (weight * inverse)
        total = term if total is None else total + term
    return total, top + jnp.log2(whole)


def iota(shape, axis):
    return lax.broadcasted_iota(jnp.int32, shape, axis)


def kernel(
    NZ, NX, NH,
    q_hbm, sk_hbm, sv_hbm, tk_hbm, tv_hbm, ids_ref, tlen_ref, plen_ref, ptab_ref,
    pk_hbm, pv_hbm, w_hbm, out_ref,
    q_raw, q_wide, sk_raw, sv_raw, tk_raw, tv_raw, pk, pv, w,
    k_sh, v_sh, k_te, v_te,
    q_all, onehot, keys, qt_send, qt_recv,
    te_m, te_l, te_own, to_send, to_recv,
    te_all, sh_o, sh_l,
    xo_send, xo_half, xo_full, zo_own, zl_own, zo_send, zo_recv,
    pr_o, pr_l, at, part, rs_recv, fx_send, final,
    in_sem,
    qz_s, qz_r, qx_s, qx_r, pair_s, pair_r, xo_s, xo_r,
    zo_s, zo_r, az_s, az_r, wx_s, wx_r, rs_s, rs_r, fx_s, fx_r,
):
    seq = lax.axis_index("seq")
    h = lax.axis_index("head")
    b = lax.rem(seq, 2)
    x = lax.rem(seq // 2, NX)
    z = seq // (2 * NX)
    pages = pk.shape[0]
    zcols = NZ * COLUMNS
    zper = NZ // NH

    def seq_of(zz, xx, bb):
        return (zz * NX + xx) * 2 + bb

    def device(zz, xx, bb, hh):
        return {"seq": seq_of(zz, xx, bb), "head": hh}

    zorder = [(p + 1) // 2 if p % 2 else -(p // 2) for p in range(NZ)]
    xorder = [0, 1, -1, 2]
    cuts = [0, 1, 5, 8] if NZ == 8 else [0, 1, NZ]
    groups = list(zip(cuts[:-1], cuts[1:]))

    def back(p):
        return [(zorder[p] + other) % NZ for other in zorder].index(0)

    def z_of(dz):
        return lax.rem(z + dz + NZ, NZ)

    def x_of(dx):
        return lax.rem(x + dx + NX, NX)

    def h_of(dh):
        return lax.rem(h + dh + NH, NH)

    def b_of(db):
        return lax.rem(b + db, 2)

    def send(src, dst, s, r, dev):
        return pltpu.make_async_remote_copy(
            src_ref=src, dst_ref=dst, send_sem=s, recv_sem=r, device_id=dev, device_id_type=MESH
        )

    me = device(z, x, b, h)
    pair = device(z, x, b_of(1), h)
    started = []

    def go(*args):
        copy = send(*args)
        copy.start()
        started.append(copy)

    def arrived(ref, s, r):
        send(ref, ref, s, r, pair).wait_recv()

    loads = {}
    for at_sem, (name, src, dst) in enumerate((
        ("q", q_hbm, q_raw),
        ("sk", sk_hbm, sk_raw.at[0]),
        ("sv", sv_hbm, sv_raw.at[0]),
        ("tk", tk_hbm, tk_raw),
        ("tv", tv_hbm, tv_raw),
        ("pk", pk_hbm, pk),
        ("pv", pv_hbm, pv),
        ("w", w_hbm, w.at[0, 0]),
    )):
        loads[name] = pltpu.make_async_copy(src, dst, in_sem.at[at_sem])
        loads[name].start()

    barrier = pltpu.get_barrier_semaphore()
    peers = [device(z_of(dz), x, b, h) for dz in range(1, NZ)]
    peers += [device(z, x_of(dx), b, h) for dx in range(1, NX)]
    peers += [
        device(z, x, b_of(db), h_of(dh)) for dh in range(NH) for db in range(2) if dh + db > 0
    ]
    for peer in peers:
        pl.semaphore_signal(barrier, inc=1, device_id=peer, device_id_type=MESH)

    loads["q"].wait()
    q_wide[...] = q_raw[...].astype(F32).reshape(R * HEADS, D)
    q_all[0, 0] = jnp.concatenate(
        [q_wide[pl.ds(i, R, stride=HEADS), :] for i in range(HEADS)], axis=0
    ).astype(BF16)

    pl.semaphore_wait(barrier, len(peers))

    left, right, far = device(z, x_of(-1), b, h), device(z, x_of(1), b, h), device(z, x_of(2), b, h)

    def z_start(buf, zs, zr, places):
        for p in places:
            q = back(p)
            go(buf.at[0, 0], buf.at[0, q], zs.at[p - 1], zr.at[q - 1], device(z_of(zorder[p]), x, b, h))

    def z_wait(buf, zs, zr, group):
        for p in range(*groups[group]):
            if p > 0:
                arrived(buf.at[0, p], zs.at[p - 1], zr.at[p - 1])

    def block(slot, group):
        first, last = groups[group]
        return q_all.at[slot, pl.ds(first, last - first)]

    def forward(group):
        for slot, to in ((2, right), (1, left), (3, far)):
            k = 3 * group + slot - 1
            go(block(0, group), block(slot, group), qx_s.at[k], qx_r.at[k], to)

    def x_wait(slot):
        for group in range(len(groups)):
            k = 3 * group + slot - 1
            arrived(block(slot, group), qx_s.at[k], qx_r.at[k])

    z_start(q_all, qz_s, qz_r, range(1, NZ))
    forward(0)
    loads["sk"].wait()
    go(sk_raw.at[0], sk_raw.at[1], pair_s.at[0], pair_r.at[0], pair)
    loads["sv"].wait()
    go(sv_raw.at[0], sv_raw.at[1], pair_s.at[1], pair_r.at[1], pair)

    row, col = iota((2 * D, 2 * D), 0), iota((2 * D, 2 * D), 1)
    sort = (col == jnp.where(row < D, 2 * row, 2 * (row - D) + 1)).astype(F32).astype(BF16)

    def sort_keys(raw, into, first, last, base):
        def step(i, carry):
            at_row = pl.multiple_of(i * 2 * D, 2 * D)
            to_row = pl.multiple_of(base + i * D, D)
            rows = dot(sort, raw[pl.ds(at_row, 2 * D), :]).astype(BF16)
            into[0, pl.ds(to_row, D), :] = rows[:D]
            into[1, pl.ds(to_row, D), :] = rows[D:]
            return carry

        lax.fori_loop(first // D, last // D, step, 0, unroll=4)

    def sort_values(raw, into, first, last, base):
        def step(i, carry):
            at_row = pl.multiple_of(i * 2 * D, 2 * D)
            to_row = pl.multiple_of(base + i * D, D)
            rows = dot(sort, raw[pl.ds(at_row, 2 * D), :])
            into[0, :, pl.ds(to_row, D)] = rows[:D].T.astype(BF16)
            into[1, :, pl.ds(to_row, D)] = rows[D:].T.astype(BF16)
            return carry

        lax.fori_loop(first // D, last // D, step, 0, unroll=4)

    positions = k_te.shape[1]
    half = sk_raw.shape[1] // 2

    tenant = seq // 4
    requests = ids_ref.shape[1]
    match = (ids_ref[...] == tenant).astype(F32)
    match = jnp.broadcast_to(match, (16, requests))
    upto = (iota((requests, requests), 0) <= iota((requests, requests), 1)).astype(F32).astype(BF16)
    slot = (match * dot(match.astype(BF16), upto)).astype(BF16)

    def mark(xx):
        j = iota((1, zcols), 1)
        place = j // COLUMNS
        away = jnp.where(place % 2 == 1, (place + 1) // 2, -(place // 2))
        aside = (xx + 1) // 2 * (1 - 2 * lax.rem(xx + 1, 2))
        owner = seq_of(lax.rem(z + away + NZ, NZ), x_of(aside), b)
        request = owner * R + lax.rem(j, R)
        pick = (iota((requests, zcols), 0) == request).astype(F32).astype(BF16)
        found = dot(slot, pick)[:1]
        group = (lax.rem(j, COLUMNS) // R).astype(F32)
        key = jnp.where(found > 0.5, group * CAP + found - 1.0, -1.0)
        keys[xx] = jnp.broadcast_to(key, (8, zcols))
        onehot[xx] = (iota((SLOTS, zcols), 0).astype(F32) == key).astype(F32).astype(BF16)

    def private(r):
        keys_here = jnp.concatenate([pk[ptab_ref[r, p]] for p in range(ptab_ref.shape[1])], axis=0)
        values_here = jnp.concatenate([pv[ptab_ref[r, p]] for p in range(ptab_ref.shape[1])], axis=0)
        s = dot_t(q_raw[r], keys_here)
        s = jnp.where(own & (lane // 2 < plen_ref[r]), s, DEAD)
        m = jnp.max(s, axis=1, keepdims=True)
        p = jnp.exp2((s - m) * SCALE)
        l = jnp.sum(p, axis=1, keepdims=True)
        o = dot(p.astype(BF16), values_here) / l
        lse = jnp.where(plen_ref[r] > 0, m * SCALE + jnp.log2(l), DEAD)
        pr_o[pl.ds(r, HEADS, stride=R), :] = o
        pr_l[pl.ds(r, HEADS, stride=R), :] = jnp.broadcast_to(lse, (HEADS, D))

    span = ptab_ref.shape[1] * pk.shape[1]
    lane = iota((HEADS, span), 1)
    own = lax.rem(lane, 2) == iota((HEADS, span), 0) // G

    def all_keys():
        loads["tk"].wait()
        sort_keys(tk_raw, k_te, 0, positions, 0)

    def own_shared():
        sort_keys(sk_raw.at[0], k_sh, 0, half, 0)
        sort_values(sv_raw.at[0], v_sh, 0, half, 0)

    def all_values():
        loads["tv"].wait()
        sort_values(tv_raw, v_te, 0, positions, 0)

    def pair_shared():
        arrived(sk_raw.at[1], pair_s.at[0], pair_r.at[0])
        sort_keys(sk_raw.at[1], k_sh, 0, half, half)
        arrived(sv_raw.at[1], pair_s.at[1], pair_r.at[1])
        sort_values(sv_raw.at[1], v_sh, 0, half, half)

    width = min(256, zcols)

    def shared(i):
        slot, c = i // (zcols // width), lax.rem(i, zcols // width)
        zs = pl.ds(c * (width // COLUMNS), width // COLUMNS)
        into = pl.ds(pl.multiple_of(c * width, width), width)
        scores = [
            dot_t(k_sh[kv], q_all[slot, zs, kv * COLUMNS:(kv + 1) * COLUMNS, :].reshape(width, D))
            for kv in range(KV)
        ]
        for kv, s in enumerate(scores):
            m = jnp.max(s, axis=0, keepdims=True)
            p = jnp.exp2((s - m) * SCALE)
            l = jnp.sum(p, axis=0, keepdims=True)
            sh_o[slot, kv, :, into] = dot(v_sh[kv], p.astype(BF16)) * (1.0 / l)
            sh_l[slot, kv, :, into] = jnp.broadcast_to(m * SCALE + jnp.log2(l), (8, width))

    per_slot = zcols // width

    def loop(first, last, body, unroll=1):
        def step(i, carry):
            body(i)
            return carry

        lax.fori_loop(first, last, step, 0, unroll=unroll)

    for slot_at in range(NX):
        mark(slot_at)
    z_wait(q_all, qz_s, qz_r, 1)
    forward(1)
    all_keys()
    for group in range(2, len(groups)):
        z_wait(q_all, qz_s, qz_r, group)
        forward(group)
    loads["w"].wait()
    go(w.at[0, 0], w.at[0, 1], pair_s.at[2], pair_r.at[2], pair)
    own_shared()
    all_values()
    loads["pk"].wait()
    loads["pv"].wait()
    for r in range(R):
        private(r)
    pair_shared()

    def chunk_queries(xx, kv):
        return q_all[xx, :, kv * COLUMNS:(kv + 1) * COLUMNS, :].reshape(zcols, D)

    found = [dot(onehot[0], chunk_queries(0, kv)) for kv in range(KV)]
    for slot_at in (2, 1, 3):
        x_wait(slot_at)
        found = [
            sums + dot(onehot[slot_at], chunk_queries(slot_at, kv)) for kv, sums in enumerate(found)
        ]
    for kv in range(KV):
        qt_send[kv] = found[kv].astype(BF16)
    go(qt_send, qt_recv, pair_s.at[3], pair_r.at[3], pair)

    go(w.at[0, 0], w.at[2, 0], wx_s.at[0], wx_r.at[0], right)
    go(w.at[0, 0], w.at[1, 0], wx_s.at[1], wx_r.at[1], left)
    loop(0, 2 * per_slot, shared)

    extent = tlen_ref[tenant] - lax.rem(seq, 4) * positions
    step_size = min(2048, positions)

    arrived(w.at[0, 1], pair_s.at[2], pair_r.at[2])
    go(w.at[0, 1], w.at[2, 1], wx_s.at[4], wx_r.at[4], right)
    go(w.at[0, 1], w.at[1, 1], wx_s.at[5], wx_r.at[5], left)
    arrived(qt_recv, pair_s.at[3], pair_r.at[3])
    for kv in range(KV):
        qt_recv[kv] = (qt_send[kv].astype(F32) + qt_recv[kv].astype(F32)).astype(BF16)
    te_m[...] = jnp.full(te_m.shape, DEAD, F32)
    te_l[...] = jnp.zeros(te_l.shape, F32)
    te_own[...] = jnp.zeros(te_own.shape, F32)

    def tenant_step(i):
        base = pl.multiple_of(i * step_size, step_size)
        scores = [dot_t(k_te[kv, pl.ds(base, step_size), :], qt_recv[kv]) for kv in range(KV)]
        for kv, s in enumerate(scores):
            s = jnp.where(iota((step_size, SLOTS), 0) < extent - base, s, DEAD)
            m_old = te_m[kv, :1]
            m = jnp.maximum(m_old, jnp.max(s, axis=0, keepdims=True))
            p = jnp.exp2((s - m) * SCALE)
            keep = jnp.exp2((m_old - m) * SCALE)
            te_m[kv, :1] = m
            te_l[kv, :1] = te_l[kv, :1] * keep + jnp.sum(p, axis=0, keepdims=True)
            te_own[kv] = te_own[kv] * keep + dot(v_te[kv, :, pl.ds(base, step_size)], p.astype(BF16))

    loop(0, positions // step_size, tenant_step)
    for kv in range(KV):
        l = te_l[kv, :1]
        o = te_own[kv] * (1.0 / l)
        lse = jnp.where(extent > 0, te_m[kv, :1] * SCALE + jnp.log2(l), DEAD)
        te_own[kv] = o
        te_l[kv, :1] = lse
        to_send[kv, :D] = o.astype(BF16)
        to_send[kv, D:] = split3(lse)
    go(to_send, to_recv, pair_s.at[4], pair_r.at[4], pair)
    loop(2 * per_slot, 4 * per_slot, shared)

    arrived(to_recv, pair_s.at[4], pair_r.at[4])
    for kv in range(KV):
        o, lse = combine([
            (te_l[kv, :1], lambda: te_own[kv]),
            (join3(to_recv[kv, D:]), lambda: to_recv[kv, :D]),
        ])
        hi = o.astype(BF16)
        te_all[kv, :D] = hi
        te_all[kv, D:2 * D] = (o - hi.astype(F32)).astype(BF16)
        te_all[kv, 2 * D:] = split3(lse)

    near = zcols // 2

    def merge(slot, side, extra=False):
        cut = pl.ds(pl.multiple_of(side * near, near), near)
        spread = onehot[slot, :, cut]
        here = keys[slot, :1, cut] >= 0.0
        height = 2 * D + STAT
        parts = dot(te_all[...].reshape(KV * height, SLOTS), spread)
        for kv in range(KV):
            own_part = parts[kv * height:(kv + 1) * height]
            lse = jnp.where(here, join3(own_part[2 * D:]), DEAD)
            pieces = [
                (sh_l[slot, kv, :1, cut], lambda: sh_o[slot, kv, :, cut]),
                (lse, lambda: own_part[:D] + own_part[D:2 * D]),
            ]
            if extra:
                pieces.append((join3(xo_half[side, kv, D:, :]), lambda: xo_half[side, kv, :D, :]))
            o, lse = combine(pieces)
            if isinstance(slot, int) and slot == 0:
                sh_o[0, kv, :, cut] = o
                sh_l[0, kv, :, cut] = jnp.broadcast_to(lse, (8, near))
            else:
                xo_send[slot - 1, kv, :D, cut] = o.astype(BF16)
                xo_send[slot - 1, kv, D:, cut] = split3(lse)

    for side, to in ((0, right), (1, left)):
        merge(3, side)
        half_cut = pl.ds(side * near, near)
        go(xo_send.at[2, :, :, half_cut], xo_half.at[side], xo_s.at[side], xo_r.at[side], to)
    for side, to in ((0, right), (1, left)):
        merge(1 + side, 1 - side)
        half_cut = pl.ds((1 - side) * near, near)
        go(xo_send.at[side, :, :, half_cut], xo_full.at[side, :, :, half_cut], xo_s.at[2 + side], xo_r.at[2 + side], to)
    loop(0, 2, lambda i: merge(0, i))
    for side, to in ((0, right), (1, left)):
        arrived(xo_half.at[side], xo_s.at[side], xo_r.at[side])
        merge(1 + side, side, True)
        half_cut = pl.ds(side * near, near)
        go(xo_send.at[side, :, :, half_cut], xo_full.at[side, :, :, half_cut], xo_s.at[4 + side], xo_r.at[4 + side], to)
    private_o = pr_o[...].T
    private_l = pr_l[...].T[:1]
    for k, side, part_at in ((2, 0, 1), (3, 1, 0), (4, 0, 0), (5, 1, 1)):
        arrived(xo_full.at[side, :, :, pl.ds(part_at * near, near)], xo_s.at[k], xo_r.at[k])

    both = 2 * COLUMNS
    low = iota((D, both), 1) < COLUMNS

    def join(i):
        cut = pl.ds(i * both, both)
        halves, marks = [], []
        for kv in range(KV):
            pieces = [(sh_l[0, kv, :1, cut], lambda: sh_o[0, kv, :, cut])]
            for side in range(2):
                pieces.append((
                    join3(xo_full[side, kv, D:, cut]),
                    lambda side=side: xo_full[side, kv, :D, cut],
                ))
            o, lse = combine(pieces)
            halves.append(o)
            marks.append(jnp.broadcast_to(lse, (8, both)))
        first_o = jnp.where(low, halves[0], pltpu.roll(halves[1], COLUMNS, 1))
        first_l = jnp.where(low[:8], marks[0], pltpu.roll(marks[1], COLUMNS, 1))
        second_o = jnp.where(low, pltpu.roll(halves[0], COLUMNS, 1), halves[1])
        second_l = jnp.where(low[:8], pltpu.roll(marks[0], COLUMNS, 1), marks[1])
        for p, o, lse in ((2 * i, first_o, first_l), (2 * i + 1, second_o, second_l)):
            zo_send[p, :D] = o.astype(BF16)
            zo_send[p, D:] = split3(lse[:1])
            if p == 0:
                zo_own[...] = o
                zl_own[...] = lse
            else:
                q = back(p)
                to = device(z_of(zorder[p]), x, b, h)
                go(zo_send.at[p], zo_recv.at[q - 1], zo_s.at[p - 1], zo_r.at[q - 1], to)

    for i in reversed(range(zcols // both)):
        join(i)

    arrived(w.at[2, 0], wx_s.at[0], wx_r.at[0])
    go(w.at[2, 0], w.at[3, 0], wx_s.at[2], wx_r.at[2], right)
    arrived(w.at[1, 1], wx_s.at[5], wx_r.at[5])
    go(w.at[1, 1], w.at[3, 1], wx_s.at[3], wx_r.at[3], left)

    pieces = [(private_l, lambda: private_o), (zl_own[:1], lambda: zo_own[...])]
    for p in range(1, NZ):
        arrived(zo_recv.at[p - 1], zo_s.at[p - 1], zo_r.at[p - 1])
        pieces.append((join3(zo_recv[p - 1, D:]), lambda p=p: zo_recv[p - 1, :D]))
    attended, _ = combine(pieces)
    at[0, 0] = attended.T.astype(BF16)

    z_start(at, az_s, az_r, reversed(range(1, NZ)))
    for group in range(len(groups)):
        z_wait(at, az_s, az_r, group)
    wide = at[0].astype(F32)
    rows = jnp.concatenate([
        wide[:, i * R:(i + 1) * R, :].reshape(NZ * R, D).astype(BF16) for i in range(HEADS)
    ], axis=1)
    arrived(w.at[2, 1], wx_s.at[4], wx_r.at[4])
    arrived(w.at[1, 0], wx_s.at[1], wx_r.at[1])
    arrived(w.at[3, 0], wx_s.at[2], wx_r.at[2])
    arrived(w.at[3, 1], wx_s.at[3], wx_r.at[3])
    def project(slot):
        sums = dot(rows, jnp.concatenate([w[slot, 0], w[slot, 1]], axis=1))
        for db in range(2):
            for p in range(NZ):
                part[db, z_of(zorder[p]), slot] = sums[p * R:(p + 1) * R, db * D:(db + 1) * D]

    loop(0, NX, project, NX)

    for k in range(1, 2 * NH):
        dh, db = k // 2, k % 2
        src = part.at[db, pl.ds(h_of(dh) * zper, zper)]
        go(src, rs_recv.at[k - 1], rs_s.at[k - 1], rs_r.at[k - 1], device(z, x, b_of(db), h_of(dh)))
    totals = [part[0, pl.ds(h * zper, zper)], None]
    for k in range(1, 2 * NH):
        arrived(rs_recv.at[k - 1], rs_s.at[k - 1], rs_r.at[k - 1])
        got = rs_recv[k - 1]
        totals[k % 2] = got if totals[k % 2] is None else totals[k % 2] + got
    first = jnp.where(b == 0, totals[0], totals[1])
    second = jnp.where(b == 0, totals[1], totals[0])

    for slot, to in ((3, far), (1, right), (2, left), (0, None)):
        rows = jnp.concatenate([first[:, slot], second[:, slot]], axis=1).astype(BF16)
        if to is None:
            final[:, x] = rows
        else:
            fx_send[slot - 1] = rows
            k = slot - 1
            go(fx_send.at[k], final.at[:, x], fx_s.at[k], fx_r.at[k], to)
    for slot, offset in ((3, 2), (1, -1), (2, 1)):
        arrived(final.at[:, x_of(offset)], fx_s.at[slot - 1], fx_r.at[slot - 1])
    out_ref[...] = final[...].reshape(zper * NX * 2 * R, D)

    for copy in started:
        copy.wait_send()


def local(NZ, NX, NH, queries, sk, sv, tk, tv, ids, tlen, plen, ptab, pk, pv, w):
    flat = lambda rows: rows.reshape(rows.shape[0] * KV, D)
    paged = lambda rows: rows.reshape(rows.shape[0], rows.shape[1] * KV, D)
    sk, sv, tk, tv = flat(sk), flat(sv), flat(tk), flat(tv)
    pk, pv = paged(pk), paged(pv)
    shared2, positions = sk.shape[0], tk.shape[0] // KV
    zcols = NZ * COLUMNS
    zper = NZ // NH
    dma = pltpu.SemaphoreType.DMA
    v = pltpu.VMEM
    scratch = [
        v(queries.shape, BF16), v((R * HEADS, D), F32),
        v((2, shared2, D), BF16), v((2, shared2, D), BF16), v(tk.shape, BF16), v(tv.shape, BF16),
        v(pk.shape, BF16), v(pv.shape, BF16), v((NX, 2) + w.shape, BF16),
        v((KV, shared2, D), BF16), v((KV, D, shared2), BF16),
        v((KV, positions, D), BF16), v((KV, D, positions), BF16),
        v((NX, NZ, R * HEADS, D), BF16), v((NX, SLOTS, zcols), BF16), v((NX, 8, zcols), F32),
        v((KV, SLOTS, D), BF16), v((KV, SLOTS, D), BF16),
        v((KV, 8, SLOTS), F32), v((KV, 8, SLOTS), F32), v((KV, D, SLOTS), F32),
        v((KV, D + STAT, SLOTS), BF16), v((KV, D + STAT, SLOTS), BF16),
        v((KV, 2 * D + STAT, SLOTS), BF16),
        v((NX, KV, D, zcols), F32), v((NX, KV, 8, zcols), F32),
        v((3, KV, D + STAT, zcols), BF16), v((2, KV, D + STAT, zcols // 2), BF16),
        v((2, KV, D + STAT, zcols), BF16),
        v((D, R * HEADS), F32), v((8, R * HEADS), F32),
        v((NZ, D + STAT, R * HEADS), BF16), v((NZ - 1, D + STAT, R * HEADS), BF16),
        v((R * HEADS, D), F32), v((R * HEADS, D), F32),
        v((1, NZ, R * HEADS, D), BF16), v((2, NZ, NX, R, D), F32),
        v((2 * NH - 1, zper, NX, R, D), F32),
        v((NX - 1, zper, 2 * R, D), BF16), v((zper, NX, 2 * R, D), BF16),
        dma((8,)),
    ]
    for count in (NZ - 1, 9, 5, 6, NZ - 1, NZ - 1, 6, 2 * NH - 1, NX - 1):
        scratch += [dma((count,)), dma((count,))]
    hbm = pl.BlockSpec(memory_space=pl.ANY)
    smem = pl.BlockSpec(memory_space=pltpu.SMEM)
    vmem = pl.BlockSpec(memory_space=pltpu.VMEM)
    return pl.pallas_call(
        functools.partial(kernel, NZ, NX, NH),
        out_shape=jax.ShapeDtypeStruct((zper * NX * 2 * R, D), BF16),
        in_specs=[hbm] * 5 + [vmem, smem, smem, smem] + [hbm] * 3,
        out_specs=vmem,
        scratch_shapes=scratch,
        compiler_params=pltpu.CompilerParams(
            collective_id=0, has_side_effects=True, vmem_limit_bytes=56 * 1024 * 1024
        ),
    )(queries, sk, sv, tk, tv, ids.reshape(1, -1), tlen, plen, ptab, pk, pv, w)


def solution(mesh):
    sizes = dict(mesh.shape)
    NX = 4
    NZ = sizes["seq"] // (2 * NX)
    placed = (
        P("seq", "head", None),
        P("seq", "head", None),
        P("seq", "head", None),
        P("seq", "head", None),
        P("seq", "head", None),
        P(),
        P(),
        P("seq"),
        P("seq", None),
        P("seq", None, "head", None),
        P("seq", None, "head", None),
        P("head", "seq"),
    )
    return jax.shard_map(
        functools.partial(local, NZ, NX, sizes["head"]),
        mesh=mesh, in_specs=placed, out_specs=P("head", "seq"), check_vma=False,
    )
```
